256 devices in a mesh: slab: 128 (over x, y_lo, z, core), member: 2 (over y_hi).
Axes of the slice: x: 4, y: 4 (y_hi: 2, y_lo: 2; y = y_hi * 2 + y_lo), z: 8, core: 2. Of those that a mesh axis runs over, the one named last changes fastest.
Arguments:
- density: bfloat16 [256, 512, 256], P('slab', 'member'), parts along dimension 1, may hold values from -6 to 6
- amplitudes: bfloat16 [256, 512, 256], P('slab', 'member'), parts along dimension 1, may hold values from 0.25 to 4
- support: int32 [256, 512, 256], P('slab', 'member'), parts along dimension 1, may hold values 0 or 1
Outputs:
- updated: bfloat16 [256, 512, 256], P('slab', 'member'), parts along dimension 1
The draws below stay inside these ranges and needn't reach their ends.
There are 2 independent parts, one for each index of `member`. The reference program is written for one: setup_inputs(seed, part) draws one part's arguments, and reference() takes and returns one part's arrays. A program takes and returns all parts, laid end to end along the dimension named above; each array names one. Nothing has to cross between parts.
Inputs may be any that keep to these rules, and one draw needn't show every extreme that they name: support holds only 0 and 1.
All inputs are finite; a program needn't handle non-finite values. No bound on the sum of `support` on one device may be relied on, other than what follows from the above.
Results may differ from the reference program's by a relative error of at most 0.0011.
Values may be sent and summed in bfloat16 or wider, within the bound.
No kernel may reach another device: no remote copies, remote signals or barrier semaphores. Data moves between devices by JAX's collectives and lax.ppermute only.
A program may use at most 64 MiB of HBM per device.

```python
import math
import jax
import jax.numpy as jnp

N = 256


def plant(result, own_key, smallest, high):
    longest = result.shape.index(max(result.shape))
    spots = []
    for shift in (0, 1):
        where = [jax.random.randint(jax.random.fold_in(own_key, axis), (), 0, length) for axis, length in enumerate(result.shape)]
        where[longest] = (where[longest] + shift) % result.shape[longest]
        spots.append(tuple(where))
    return result.at[spots[0]].set(smallest).at[spots[1]].set(high)


def shard_levels(own_key, dims, pieces, least, high):
    loudness, own = 1.0, jax.random.fold_in(own_key, 6)
    for dim, parts in pieces:
        draws = jnp.exp(jax.random.uniform(jax.random.fold_in(own, dim), (parts,), jnp.float32, least / len(pieces), high / len(pieces)))
        loudness = loudness * jnp.repeat(draws, dims[dim] // parts).reshape([-1 if axis == dim else 1 for axis in range(len(dims))])
    return loudness


def centred(stream_key, shape, deviation, bound, split=(), kind=jnp.bfloat16):
    result = jax.random.normal(stream_key, shape, jnp.float32) * deviation
    if len(split) > 0:
        result = shard_levels(stream_key, shape, split, -0.22, 0.18) * result
    return jnp.clip(result, min=-bound, max=bound).astype(kind)


def setup_inputs(seed: int = 0, part: int = 0) -> dict:
    arg_keys = jax.random.split(jax.random.key(seed), 4)
    part_keys = jax.random.split(jax.random.fold_in(arg_keys[3], part), 4)
    density = centred(part_keys[0], (N, N, N), 1.0, 6.0, ((0, 128),))
    amplitudes = jnp.clip(jnp.exp(math.log(4.0) - 2.7725887 * jax.random.uniform(part_keys[1], (N, N, N), jnp.float32) ** shard_levels(part_keys[1], (N, N, N), ((0, 128),), -0.2, 0.2)), 0.25, 4.0).astype(jnp.bfloat16)
    support = plant((jax.random.randint(part_keys[2], (N, N, N), 0, 2) < 1).astype(jnp.int32), jax.random.fold_in(part_keys[2], 1), 0, 1)
    return {"density": density, "amplitudes": amplitudes, "support": support}


modulus_floor = 0.25

def shift_angle(length):
    positions = jnp.arange(length, dtype=jnp.int32)
    return ((length - 1) * positions % (2 * length)).astype(jnp.float32) * (math.pi / length)

def reference(density, amplitudes, support):
    rho = density.astype(jnp.float32)
    angle = shift_angle(N)
    phase = jnp.cos(angle) + 1j * jnp.sin(angle)
    field = rho * phase[None, None, :]
    field = field * phase[None, :, None]
    field = field * phase[:, None, None]
    spectrum = jnp.fft.fftn(field) / (N * math.sqrt(N))
    target = 0.5 * (amplitudes.astype(jnp.float32) + amplitudes[::-1, ::-1, ::-1].astype(jnp.float32))
    magnitude = jnp.sqrt(spectrum.real * spectrum.real + spectrum.imag * spectrum.imag)
    projected = spectrum * (target / jnp.maximum(magnitude, modulus_floor))
    field = jnp.fft.ifftn(projected) * (N * math.sqrt(N))
    back = jnp.conj(phase)
    field = field * back[None, None, :]
    field = field * back[None, :, None]
    field = field * back[:, None, None]
    moduled = field.real
    mask = support.astype(jnp.float32)
    updated = rho + mask * (2.0 * moduled - rho) - moduled
    return updated.astype(jnp.bfloat16)
```

```python
import functools

import jax
import jax.numpy as jnp
import ml_dtypes
import numpy as np
from jax import lax
from jax.experimental import pallas as pl
from jax.experimental.pallas import tpu as pltpu
from jax.sharding import PartitionSpec as P

N = 256
CHIPS = 64
HALF = N // 2
QUARTER = N // 4
FLOOR = 0.25
FULL = 8190.0
FORWARD_LOW = -4
INVERSE_LOW = -9
AMP_UNIT = 512.0


def angles(k, position):
    turns = np.outer(2 * np.asarray(k) - (N - 1), np.asarray(position)) % (2 * N)
    return turns * (np.pi / N)


def split(table):
    high = table.astype(ml_dtypes.bfloat16)
    low = (table - high.astype(np.float64)).astype(ml_dtypes.bfloat16)
    return high, low


def two(tables):
    highs, lows = zip(*(split(t) for t in tables))
    return np.stack(highs), np.stack(lows)


@functools.cache
def constants():
    out = {}
    scale = 1.0 / np.sqrt(N)
    every = np.arange(N)
    half = np.arange(HALF)
    forward, inverse = [], []
    for core in range(2):
        kx = np.tile(np.arange(QUARTER) + QUARTER * core, 2)
        a = angles(kx, every)
        forward.append(np.concatenate([np.cos(a), -np.sin(a)], 0).T * scale)
        inverse.append(np.concatenate([np.cos(a), -np.sin(a)], 0) * (2.0 * scale))
    out["tx"] = two(forward)
    out["txi"] = two(inverse)
    a = angles(half, every)
    out["ty"] = split(np.concatenate([np.cos(a), np.sin(a)], 0) * scale)
    out["tyi"] = split(np.concatenate([np.cos(a), np.sin(a)], 0).T * scale)
    forward, inverse = [], []
    for core in range(2):
        planes = [0, 1, 2, 3] if core == 0 else [2, 3, 0, 1]
        z = np.concatenate([4 * np.arange(CHIPS) + p for p in planes])
        a = angles(z, z)
        forward.append(np.concatenate([np.cos(a), np.sin(a)], 0) * scale)
        inverse.append(np.concatenate([np.cos(a.T), np.sin(a.T)], 0) * scale)
    out["tz"] = two(forward)
    out["tzi"] = two(inverse)
    picks = []
    for core in range(2):
        pick = np.zeros((2 * N, 2 * HALF))
        for h in range(2):
            for j in range(QUARTER):
                kx = QUARTER * core + j
                pick[N * h + kx, QUARTER * h + j] = 1
                pick[N * (1 - h) + N - 1 - kx, HALF + QUARTER * h + j] = 1
        picks.append(pick)
    out["pick"] = np.stack(picks).astype(ml_dtypes.bfloat16)
    out["rev_half"] = np.eye(HALF)[::-1].astype(ml_dtypes.bfloat16)
    out["rev_all"] = np.eye(N)[::-1].astype(ml_dtypes.bfloat16)
    return out


def mm(a, b):
    return jnp.dot(a, b, preferred_element_type=jnp.float32)


def cut(x):
    high = x.astype(jnp.bfloat16)
    return high, (x - high.astype(jnp.float32)).astype(jnp.bfloat16)


def left3(high, low, x):
    xh, xl = cut(x)
    return mm(high, xh) + (mm(high, xl) + mm(low, xh))


def right3(x, high, low):
    xh, xl = cut(x)
    return mm(xh, high) + (mm(xl, high) + mm(xh, low))


def pack(re, im, low):
    m = jnp.maximum(jnp.maximum(jnp.abs(re), jnp.abs(im)), 1e-30)
    e = jnp.clip(jnp.floor(jnp.log2(m)) + (1.0 - low), 0.0, 15.0)
    s = jnp.exp2(-(e + low)) * FULL
    a = jnp.floor(re * s + 0.5).astype(jnp.int32)
    b = jnp.floor(im * s + 0.5).astype(jnp.int32)
    return (a << 18) | ((b & 0x3FFF) << 4) | e.astype(jnp.int32)


def unpack(word, low):
    s = jnp.exp2((word & 15).astype(jnp.float32) + low) * (1.0 / FULL)
    re = (word >> 18).astype(jnp.float32) * s
    im = ((word << 14) >> 18).astype(jnp.float32) * s
    return re, im


def signs(y_axis_len):
    y = lax.broadcasted_iota(jnp.int32, (y_axis_len, 2 * HALF), 0)
    lane = lax.broadcasted_iota(jnp.int32, (y_axis_len, 2 * HALF), 1)
    odd = (y & 1) * ((lane >> 6) & 1)
    return (1 - 2 * odd).astype(jnp.float32)


def forward_kernel(core_ref, own, other, amp_own, amp_other, txh, txl, tyh, tyl, pick, rev, out):
    core = core_ref[0]
    sign = signs(N)
    table_high, table_low = txh[core], txl[core]
    chosen = pick[core]
    for p in range(4):
        rho = (own if p < 2 else other)[p % 2]
        a = (mm(rho, table_high) + mm(rho, table_low)) * sign
        u = left3(tyh[...], tyl[...], a)
        re = u[:HALF, :HALF] + u[HALF:, HALF:]
        im = u[:HALF, HALF:] - u[HALF:, :HALF]
        word = pack(re, im, FORWARD_LOW)
        amp = (amp_own if p < 2 else amp_other)[p % 2]
        both = mm(jnp.concatenate([amp[:HALF], amp[HALF:]], 1), chosen)
        direct = both[:, :HALF]
        mirror = mm(rev[...], both[:, HALF:].astype(jnp.bfloat16))
        coded = ((direct * AMP_UNIT).astype(jnp.int32) << 16) | (mirror * AMP_UNIT).astype(jnp.int32)
        for r in range(2):
            rows = slice(CHIPS * r, CHIPS * (r + 1))
            out[pl.ds(2 * p + r, CHIPS, stride=16), :] = word[rows]
            out[pl.ds(8 + 2 * p + r, CHIPS, stride=16), :] = coded[rows]


def middle_kernel(core_ref, msg, tzh, tzl, tzih, tzil, rev, out):
    core = core_ref[0]

    def gather(first):
        return jnp.concatenate(
            [
                jnp.concatenate(
                    [msg[pl.ds(first + 2 * p + r, CHIPS, stride=16), :] for p in range(4)], 0
                )
                for r in range(2)
            ],
            1,
        )

    re, im = unpack(gather(0), FORWARD_LOW)
    u = left3(tzh[core], tzl[core], jnp.concatenate([re, im], 1))
    re = u[:N, :N] + u[N:, N:]
    im = u[:N, N:] - u[N:, :N]
    coded = gather(8)
    direct = (coded >> 16).astype(jnp.float32)
    mirror = mm(rev[...], (coded & 0xFFFF).astype(jnp.float32).astype(jnp.bfloat16))
    target = (direct + mirror) * (0.5 / AMP_UNIT)
    ratio = target / jnp.maximum(jnp.sqrt(re * re + im * im), FLOOR)
    u = left3(tzih[core], tzil[core], jnp.concatenate([re * ratio, im * ratio], 1))
    word = pack(u[:N, :N] - u[N:, N:], u[:N, N:] + u[N:, :N], INVERSE_LOW)
    for p in range(4):
        for r in range(2):
            out[pl.ds(2 * p + r, CHIPS, stride=8), :] = word[
                CHIPS * p : CHIPS * (p + 1), HALF * r : HALF * (r + 1)
            ]


def inverse_kernel(core_ref, own, other, rho_ref, support, tyh, tyl, txh, txl, out):
    core = core_ref[0]
    sign = signs(N)
    for q in range(2):
        moduled = None
        for part, (ref, first, c) in enumerate(((own, 2 * q, core), (other, 4 + 2 * q, 1 - core))):
            word = jnp.concatenate(
                [ref[pl.ds(first + r, CHIPS, stride=8), :] for r in range(2)], 0
            )
            re, im = unpack(word, INVERSE_LOW)
            g = jnp.concatenate(
                [jnp.concatenate([re, im], 1), jnp.concatenate([-im, re], 1)], 0
            )
            lines = left3(tyh[...], tyl[...], g) * sign
            term = right3(lines, txh[c], txl[c])
            moduled = term if moduled is None else moduled + term
        rho = rho_ref[q].astype(jnp.float32)
        mask = support[q].astype(jnp.float32)
        out[q] = (rho + mask * (2.0 * moduled - rho) - moduled).astype(jnp.bfloat16)


def call(kernel, out_shape, core, *operands):
    return pl.pallas_call(
        kernel,
        out_shape=out_shape,
        in_specs=[pl.BlockSpec(memory_space=pltpu.SMEM)]
        + [pl.BlockSpec(memory_space=pltpu.VMEM)] * len(operands),
        out_specs=pl.BlockSpec(memory_space=pltpu.VMEM),
        compiler_params=pltpu.CompilerParams(vmem_limit_bytes=48 * 2**20),
    )(core, *operands)


def shards(density, amplitudes, support):
    c = {k: jax.tree.map(jnp.asarray, v) for k, v in constants().items()}
    swap = [(i, i ^ 1) for i in range(2 * CHIPS)]
    same_core = [list(range(core, 2 * CHIPS, 2)) for core in range(2)]
    core = (lax.axis_index("slab") % 2).astype(jnp.int32).reshape(1)

    def exchange(x):
        return lax.all_to_all(
            x, "slab", split_axis=0, concat_axis=0, tiled=True, axis_index_groups=same_core
        )

    density_other = lax.ppermute(density, "slab", swap)
    amplitudes_other = lax.ppermute(amplitudes, "slab", swap)
    sent = call(
        forward_kernel,
        jax.ShapeDtypeStruct((CHIPS * 16, HALF), jnp.int32),
        core, density, density_other, amplitudes, amplitudes_other,
        *c["tx"], *c["ty"], c["pick"], c["rev_half"],
    )
    lines = exchange(sent.reshape(CHIPS, 16, HALF)).reshape(CHIPS * 16, HALF)
    sent = call(
        middle_kernel,
        jax.ShapeDtypeStruct((CHIPS * 8, HALF), jnp.int32),
        core, lines, *c["tz"], *c["tzi"], c["rev_all"],
    )
    planes = exchange(sent.reshape(CHIPS, 8, HALF)).reshape(CHIPS * 8, HALF)
    planes_other = lax.ppermute(planes, "slab", swap)
    return call(
        inverse_kernel,
        jax.ShapeDtypeStruct(density.shape, jnp.bfloat16),
        core, planes, planes_other, density, support, *c["tyi"], *c["txi"],
    )


def solution(mesh):
    spec = P("slab", "member", None)
    return jax.shard_map(
        shards, mesh=mesh, in_specs=(spec, spec, spec), out_specs=spec, check_vma=False
    )
```

```python
import functools

import jax
import jax.numpy as jnp
import ml_dtypes
import numpy as np
from jax import lax
from jax.experimental import pallas as pl
from jax.experimental.pallas import tpu as pltpu
from jax.sharding import PartitionSpec as P

N = 256
CHIPS = 64
HALF = N // 2
QUARTER = N // 4
FLOOR = 0.25
FULL = 16380.0
FORWARD_LOW = -20
INVERSE_LOW = -25
AMP_UNIT = 512.0


def angles(k, position):
    turns = np.outer(2 * np.asarray(k) - (N - 1), np.asarray(position)) % (2 * N)
    return turns * (np.pi / N)


def split(table):
    high = table.astype(ml_dtypes.bfloat16)
    low = (table - high.astype(np.float64)).astype(ml_dtypes.bfloat16)
    return high, low


def two(tables):
    highs, lows = zip(*(split(t) for t in tables))
    return np.stack(highs), np.stack(lows)


@functools.cache
def constants():
    out = {}
    scale = 1.0 / np.sqrt(N)
    every = np.arange(N)
    half = np.arange(HALF)
    forward, inverse = [], []
    for core in range(2):
        kx = np.tile(np.arange(QUARTER) + QUARTER * core, 2)
        a = angles(kx, every)
        forward.append(np.concatenate([np.cos(a), -np.sin(a)], 0).T * scale)
        inverse.append(np.concatenate([np.cos(a), -np.sin(a)], 0) * (2.0 * scale))
    out["tx"] = np.stack([np.concatenate(split(t), 1) for t in forward])
    out["txi"] = two(inverse)
    a = angles(half, every)
    out["ty"] = np.concatenate(split(np.concatenate([np.cos(a), np.sin(a)], 0) * scale), 0)
    out["tyi"] = split(np.concatenate([np.cos(a), np.sin(a)], 0).T * scale)
    forward, inverse = [], []
    for core in range(2):
        planes = [0, 1, 2, 3] if core == 0 else [2, 3, 0, 1]
        z = np.concatenate([4 * np.arange(CHIPS) + p for p in planes])
        a = angles(z, z)
        forward.append(np.concatenate([np.cos(a), np.sin(a)], 0) * scale)
        inverse.append(np.concatenate([np.cos(a.T), np.sin(a.T)], 0) * scale)
    out["tz"] = two(forward)
    out["tzi"] = two(inverse)
    picks = []
    for core in range(2):
        pick = np.zeros((2 * N, 2 * HALF))
        for h in range(2):
            for j in range(QUARTER):
                kx = QUARTER * core + j
                pick[N * h + kx, QUARTER * h + j] = 1
                pick[N * (1 - h) + N - 1 - kx, HALF + QUARTER * h + j] = 1
        picks.append(pick)
    out["pick"] = np.stack(picks).astype(ml_dtypes.bfloat16)
    out["rev_half"] = np.eye(HALF)[::-1].astype(ml_dtypes.bfloat16)
    out["rev_all"] = np.eye(N)[::-1].astype(ml_dtypes.bfloat16)
    return out


def mm(a, b):
    return jnp.dot(a, b, preferred_element_type=jnp.float32)


def cut(x):
    high = x.astype(jnp.bfloat16)
    return high, (x - high.astype(jnp.float32)).astype(jnp.bfloat16)


def left3(high, low, x):
    xh, xl = cut(x)
    return mm(high, xh) + (mm(high, xl) + mm(low, xh))


def right3(x, high, low):
    xh, xl = cut(x)
    return mm(xh, high) + (mm(xl, high) + mm(xh, low))


def pack(re0, im0, re1, im1, low):
    m = jnp.maximum(jnp.maximum(jnp.abs(re0), jnp.abs(im0)), jnp.maximum(jnp.abs(re1), jnp.abs(im1)))
    e = jnp.clip(jnp.floor(jnp.log2(jnp.maximum(m, 1e-30))) + (1.0 - low), 0.0, 31.0)
    s = jnp.exp2(-(e + low)) * FULL
    e = e.astype(jnp.int32)

    def code(x, factor):
        return jnp.floor(x * factor + 0.5).astype(jnp.int32)

    word0 = (code(re0, s) << 17) | ((code(im0, s) & 0x7FFF) << 2) | (e & 3)
    word1 = (code(re1, s) << 17) | ((code(im1, 0.5 * s) & 0x3FFF) << 3) | (e >> 2)
    return word0, word1


def unpack(word0, word1, low):
    e = (word0 & 3) | ((word1 & 7) << 2)
    s = jnp.exp2(e.astype(jnp.float32) + low) * (1.0 / FULL)
    re0 = (word0 >> 17).astype(jnp.float32) * s
    im0 = ((word0 << 15) >> 17).astype(jnp.float32) * s
    re1 = (word1 >> 17).astype(jnp.float32) * s
    im1 = ((word1 << 15) >> 18).astype(jnp.float32) * (2.0 * s)
    return re0, im0, re1, im1


def signs(y_axis_len):
    y = lax.broadcasted_iota(jnp.int32, (y_axis_len, 2 * HALF), 0)
    lane = lax.broadcasted_iota(jnp.int32, (y_axis_len, 2 * HALF), 1)
    odd = (y & 1) * ((lane >> 6) & 1)
    return (1 - 2 * odd).astype(jnp.float32)


def forward_planes(first, rho_ref, amp_ref, tx, ty, pick, rev, out, ready):
    sign = signs(N)
    ready("rho", "tx")
    lines = []
    for q in range(2):
        a = mm(rho_ref[q], tx[...])
        lines.append((a[:, :N] + a[:, N:]) * sign)
    ready("ty")
    parts = []
    for a in lines:
        u = left3(ty[:N], ty[N:], a)
        parts += [u[:HALF, :HALF] + u[HALF:, HALF:], u[:HALF, HALF:] - u[HALF:, :HALF]]
    words = pack(*parts, FORWARD_LOW)
    ready("amp", "pick", "rev")
    for q in range(2):
        amp = amp_ref[q]
        both = mm(jnp.concatenate([amp[:HALF], amp[HALF:]], 1), pick[...])
        direct = both[:, :HALF]
        mirror = mm(rev[...], both[:, HALF:].astype(jnp.bfloat16))
        coded = ((direct * AMP_UNIT).astype(jnp.int32) << 16) | (mirror * AMP_UNIT).astype(jnp.int32)
        for r in range(2):
            rows = slice(CHIPS * r, CHIPS * (r + 1))
            slot = 2 * (first + q) + r
            out[pl.ds(slot, CHIPS, stride=16), :] = words[q][rows]
            out[pl.ds(8 + slot, CHIPS, stride=16), :] = coded[rows]


def first_kernel(core_ref, rho_hbm, amp_hbm, tx_hbm, ty_hbm, pick_hbm, rev_hbm,
                 out, tx, ty, pick, rev, rho, amp, sems):
    core = core_ref[0]
    copies = {}
    for i, (name, source, target) in enumerate((
        ("rho", rho_hbm, rho),
        ("tx", tx_hbm.at[core], tx),
        ("ty", ty_hbm, ty),
        ("amp", amp_hbm, amp),
        ("pick", pick_hbm.at[core], pick),
        ("rev", rev_hbm, rev),
    )):
        copies[name] = pltpu.make_async_copy(source, target, sems.at[i])
        copies[name].start()

    def ready(*names):
        for name in names:
            copies[name].wait()

    forward_planes(0, rho, amp, tx, ty, pick, rev, out, ready)


def second_kernel(sent, rho, amp, tx, ty, pick, rev, out):
    forward_planes(2, rho, amp, tx, ty, pick, rev, out, lambda *names: None)


def middle_kernel(core_ref, msg, tzh, tzl, tzih, tzil, rev, out):
    core = core_ref[0]
    for r in range(2):

        def rows(slot):
            return msg[pl.ds(slot + r, CHIPS, stride=16), :]

        re, im = [], []
        for p in (0, 2):
            re0, im0, re1, im1 = unpack(rows(2 * p), rows(2 * p + 2), FORWARD_LOW)
            re += [re0, re1]
            im += [im0, im1]
        lines = jnp.concatenate([jnp.concatenate(re, 0), jnp.concatenate(im, 0)], 1)
        u = left3(tzh[core], tzl[core], lines)
        re = u[:N, :HALF] + u[N:, HALF:]
        im = u[:N, HALF:] - u[N:, :HALF]
        coded = jnp.concatenate([rows(8 + 2 * p) for p in range(4)], 0)
        direct = (coded >> 16).astype(jnp.float32)
        mirror = mm(rev[...], (coded & 0xFFFF).astype(jnp.float32).astype(jnp.bfloat16))
        target = (direct + mirror) * (0.5 / AMP_UNIT)
        ratio = target / jnp.maximum(jnp.sqrt(re * re + im * im), FLOOR)
        u = left3(tzih[core], tzil[core], jnp.concatenate([re * ratio, im * ratio], 1))
        re = u[:N, :HALF] - u[N:, HALF:]
        im = u[:N, HALF:] + u[N:, :HALF]
        for p in (0, 2):
            planes = [slice(CHIPS * i, CHIPS * (i + 1)) for i in (p, p + 1)]
            words = pack(re[planes[0]], im[planes[0]], re[planes[1]], im[planes[1]], INVERSE_LOW)
            for i in range(2):
                out[pl.ds(2 * (p + i) + r, CHIPS, stride=8), :] = words[i]


def half_planes(ref, first, tyh, tyl, txh, txl):
    sign = signs(N)
    words = [
        jnp.concatenate([ref[pl.ds(2 * p + r, CHIPS, stride=8), :] for r in range(2)], 0)
        for p in (first, first + 1)
    ]
    parts = unpack(*words, INVERSE_LOW)
    out = []
    for q in range(2):
        re, im = parts[2 * q : 2 * q + 2]
        g = jnp.concatenate([jnp.concatenate([re, im], 1), jnp.concatenate([-im, re], 1)], 0)
        out.append(right3(left3(tyh[...], tyl[...], g) * sign, txh, txl))
    return out


def own_kernel(core_ref, own, tyh, tyl, txh, txl, out):
    core = core_ref[0]
    for q, term in enumerate(half_planes(own, 0, tyh, tyl, txh[core], txl[core])):
        out[q] = term


def update_kernel(core_ref, partial, other, rho_ref, support, tyh, tyl, txh, txl, out):
    core = 1 - core_ref[0]
    for q, term in enumerate(half_planes(other, 2, tyh, tyl, txh[core], txl[core])):
        moduled = partial[q] + term
        rho = rho_ref[q].astype(jnp.float32)
        mask = support[q].astype(jnp.float32)
        out[q] = (rho + mask * (2.0 * moduled - rho) - moduled).astype(jnp.bfloat16)


SMEM = pl.BlockSpec(memory_space=pltpu.SMEM)
VMEM = pl.BlockSpec(memory_space=pltpu.VMEM)
HBM = pl.BlockSpec(memory_space=pltpu.HBM)


def call(kernel, out_shape, operands, in_specs, flops, **more):
    return pl.pallas_call(
        kernel,
        out_shape=out_shape,
        in_specs=in_specs,
        out_specs=jax.tree.map(lambda _: VMEM, out_shape),
        compiler_params=pltpu.CompilerParams(vmem_limit_bytes=40 * 2**20),
        cost_estimate=pl.CostEstimate(
            flops=int(flops), bytes_accessed=2 * 2**20, transcendentals=0
        ),
        **more,
    )(*operands)


def shards(density, amplitudes, support):
    c = {k: jax.tree.map(jnp.asarray, v) for k, v in constants().items()}
    swap = [(i, i ^ 1) for i in range(2 * CHIPS)]
    same_core = [list(range(core, 2 * CHIPS, 2)) for core in range(2)]
    core = (lax.axis_index("slab") % 2).astype(jnp.int32).reshape(1)

    def exchange(x):
        return lax.all_to_all(
            x, "slab", split_axis=0, concat_axis=0, tiled=True, axis_index_groups=same_core
        )

    def shape(dims, kind):
        return jax.ShapeDtypeStruct(dims, kind)

    density_other = lax.ppermute(density, "slab", swap)
    amplitudes_other = lax.ppermute(amplitudes, "slab", swap)
    message = shape((CHIPS * 16, HALF), jnp.int32)
    kept = [
        shape(c["tx"].shape[1:], jnp.bfloat16),
        shape(c["ty"].shape, jnp.bfloat16),
        shape(c["pick"].shape[1:], jnp.bfloat16),
        shape(c["rev_half"].shape, jnp.bfloat16),
    ]
    sent, *tables = call(
        first_kernel,
        [message, *kept],
        (core, density, amplitudes, c["tx"], c["ty"], c["pick"], c["rev_half"]),
        [SMEM] + [HBM] * 6,
        400e6,
        scratch_shapes=[
            pltpu.VMEM(density.shape, jnp.bfloat16),
            pltpu.VMEM(density.shape, jnp.bfloat16),
            pltpu.SemaphoreType.DMA((6,)),
        ],
    )
    sent = call(
        second_kernel,
        message,
        (sent, density_other, amplitudes_other, *tables),
        [VMEM] * 7,
        400e6,
        input_output_aliases={0: 0},
    )
    lines = exchange(sent.reshape(CHIPS, 16, HALF)).reshape(CHIPS * 16, HALF)
    sent = call(
        middle_kernel,
        shape((CHIPS * 8, HALF), jnp.int32),
        (core, lines, *c["tz"], *c["tzi"], c["rev_all"]),
        [SMEM] + [VMEM] * 6,
        800e6,
    )
    planes = exchange(sent.reshape(CHIPS, 8, HALF)).reshape(CHIPS * 8, HALF)
    planes_other = lax.ppermute(planes, "slab", swap)
    tables = (*c["tyi"], *c["txi"])
    partial = call(
        own_kernel,
        shape(density.shape, jnp.float32),
        (core, planes, *tables),
        [SMEM] + [VMEM] * 5,
        400e6,
    )
    return call(
        update_kernel,
        shape(density.shape, jnp.bfloat16),
        (core, partial, planes_other, density, support, *tables),
        [SMEM] + [VMEM] * 8,
        400e6,
    )


def solution(mesh):
    spec = P("slab", "member", None)
    return jax.shard_map(
        shards, mesh=mesh, in_specs=(spec, spec, spec), out_specs=spec, check_vma=False
    )
```

```python
import functools

import jax
import jax.numpy as jnp
import ml_dtypes
import numpy as np
from jax import lax
from jax.experimental import pallas as pl
from jax.experimental.pallas import tpu as pltpu
from jax.sharding import PartitionSpec as P

N = 256
CHIPS = 64
HALF = N // 2
QUARTER = N // 4
FLOOR = 0.25
FULL = 16380.0
FORWARD_LOW = -20
INVERSE_LOW = -25
AMP_UNIT = 512.0
ORDER = np.arange(CHIPS) ^ 44


def angles(k, position):
    turns = np.outer(2 * np.asarray(k) - (N - 1), np.asarray(position)) % (2 * N)
    return turns * (np.pi / N)


def split(table):
    high = table.astype(ml_dtypes.bfloat16)
    low = (table - high.astype(np.float64)).astype(ml_dtypes.bfloat16)
    return high, low


def two(tables):
    highs, lows = zip(*(split(t) for t in tables))
    return np.stack(highs), np.stack(lows)


@functools.cache
def constants():
    out = {}
    scale = 1.0 / np.sqrt(N)
    every = np.arange(N)
    half = np.arange(HALF)
    forward, inverse = [], []
    for core in range(2):
        kx = np.tile(np.arange(QUARTER) + QUARTER * core, 2)
        a = angles(kx, every)
        forward.append(np.concatenate([np.cos(a), -np.sin(a)], 0).T * scale)
        inverse.append(np.concatenate([np.cos(a), -np.sin(a)], 0) * (2.0 * scale))
    tx = forward
    out["txi"] = two(inverse)
    a = angles(half, every)
    ty = np.concatenate([np.cos(a), np.sin(a)], 0) * scale
    out["tyi"] = split(np.concatenate([np.cos(a), np.sin(a)], 0).T * scale)
    forward, inverse = [], []
    for core in range(2):
        planes = [0, 1, 2, 3] if core == 0 else [2, 3, 0, 1]
        z = np.concatenate([4 * ORDER + p for p in planes])
        a = angles(z, z)
        forward.append(np.concatenate([np.cos(a), np.sin(a)], 0) * scale)
        inverse.append(np.concatenate([np.cos(a.T), np.sin(a.T)], 0) * scale)
    out["tz"] = two(forward)
    out["tzi"] = two(inverse)
    picks = []
    for core in range(2):
        pick = np.zeros((2 * N, 2 * HALF))
        for h in range(2):
            for j in range(QUARTER):
                kx = QUARTER * core + j
                pick[N * h + kx, QUARTER * h + j] = 1
                pick[N * (1 - h) + N - 1 - kx, HALF + QUARTER * h + j] = 1
        picks.append(pick)
    rev = np.zeros((HALF, N))
    rev[:, :HALF] = np.eye(HALF)[::-1]
    out["first"] = np.stack(
        [
            np.concatenate([*split(tx[core]), *split(ty), picks[core], rev], 0).astype(ml_dtypes.bfloat16)
            for core in range(2)
        ]
    )
    out["rev_all"] = np.eye(N)[::-1].astype(ml_dtypes.bfloat16)
    return out


def mm(a, b):
    return jnp.dot(a, b, preferred_element_type=jnp.float32)


def cut(x):
    high = x.astype(jnp.bfloat16)
    return high, (x - high.astype(jnp.float32)).astype(jnp.bfloat16)


def left3(high, low, x):
    xh, xl = cut(x)
    return mm(high, xh) + (mm(high, xl) + mm(low, xh))


def right3(x, high, low):
    xh, xl = cut(x)
    return mm(xh, high) + (mm(xl, high) + mm(xh, low))


def pack(re0, im0, re1, im1, low):
    m = jnp.maximum(jnp.maximum(jnp.abs(re0), jnp.abs(im0)), jnp.maximum(jnp.abs(re1), jnp.abs(im1)))
    e = jnp.clip(jnp.floor(jnp.log2(jnp.maximum(m, 1e-30))) + (1.0 - low), 0.0, 31.0)
    s = jnp.exp2(-(e + low)) * FULL
    e = e.astype(jnp.int32)

    def code(x, factor):
        return jnp.floor(x * factor + 0.5).astype(jnp.int32)

    word0 = (code(re0, s) << 17) | ((code(im0, s) & 0x7FFF) << 2) | (e & 3)
    word1 = (code(re1, s) << 17) | ((code(im1, 0.5 * s) & 0x3FFF) << 3) | (e >> 2)
    return word0, word1


def unpack(word0, word1, low):
    e = (word0 & 3) | ((word1 & 7) << 2)
    s = jnp.exp2(e.astype(jnp.float32) + low) * (1.0 / FULL)
    re0 = (word0 >> 17).astype(jnp.float32) * s
    im0 = ((word0 << 15) >> 17).astype(jnp.float32) * s
    re1 = (word1 >> 17).astype(jnp.float32) * s
    im1 = ((word1 << 15) >> 18).astype(jnp.float32) * (2.0 * s)
    return re0, im0, re1, im1


def signs(y_axis_len):
    y = lax.broadcasted_iota(jnp.int32, (y_axis_len, 2 * HALF), 0)
    lane = lax.broadcasted_iota(jnp.int32, (y_axis_len, 2 * HALF), 1)
    odd = (y & 1) * ((lane >> 6) & 1)
    return (1 - 2 * odd).astype(jnp.float32)


def forward_planes(first, rho_ref, amp_ref, table, out):
    sign = signs(N)
    parts = []
    for q in range(2):
        a = mm(rho_ref[q], table[:N]) + mm(rho_ref[q], table[N : 2 * N])
        u = left3(table[2 * N : 3 * N], table[3 * N : 4 * N], a * sign)
        parts += [u[:HALF, :HALF] + u[HALF:, HALF:], u[:HALF, HALF:] - u[HALF:, :HALF]]
    words = pack(*parts, FORWARD_LOW)
    for q in range(2):
        amp = amp_ref[q]
        both = mm(jnp.concatenate([amp[:HALF], amp[HALF:]], 1), table[4 * N : 6 * N])
        direct = both[:, :HALF]
        mirror = mm(table[6 * N :, :HALF], both[:, HALF:].astype(jnp.bfloat16))
        coded = ((direct * AMP_UNIT).astype(jnp.int32) << 16) | (mirror * AMP_UNIT).astype(jnp.int32)
        for r in range(2):
            rows = slice(CHIPS * r, CHIPS * (r + 1))
            slot = 2 * (first + q) + r
            out[pl.ds(slot, CHIPS, stride=16), :] = words[q][rows]
            out[pl.ds(8 + slot, CHIPS, stride=16), :] = coded[rows]


def forward_kernel(own, rho_other, amp_other, table, out):
    forward_planes(0, own.at[:2], own.at[2:], table, out)
    forward_planes(2, rho_other, amp_other, table, out)


def middle_kernel(core_ref, msg, tzh, tzl, tzih, tzil, rev, out):
    core = core_ref[0]
    for r in range(2):

        def rows(slot):
            return msg[pl.ds(slot + r, CHIPS, stride=16), :]

        re, im = [], []
        for p in (0, 2):
            re0, im0, re1, im1 = unpack(rows(2 * p), rows(2 * p + 2), FORWARD_LOW)
            re += [re0, re1]
            im += [im0, im1]
        lines = jnp.concatenate([jnp.concatenate(re, 0), jnp.concatenate(im, 0)], 1)
        u = left3(tzh[core], tzl[core], lines)
        re = u[:N, :HALF] + u[N:, HALF:]
        im = u[:N, HALF:] - u[N:, :HALF]
        coded = jnp.concatenate([rows(8 + 2 * p) for p in range(4)], 0)
        direct = (coded >> 16).astype(jnp.float32)
        mirror = mm(rev[...], (coded & 0xFFFF).astype(jnp.float32).astype(jnp.bfloat16))
        target = (direct + mirror) * (0.5 / AMP_UNIT)
        ratio = target / jnp.maximum(jnp.sqrt(re * re + im * im), FLOOR)
        u = left3(tzih[core], tzil[core], jnp.concatenate([re * ratio, im * ratio], 1))
        re = u[:N, :HALF] - u[N:, HALF:]
        im = u[:N, HALF:] + u[N:, :HALF]
        for p in (0, 2):
            planes = [slice(CHIPS * i, CHIPS * (i + 1)) for i in (p, p + 1)]
            words = pack(re[planes[0]], im[planes[0]], re[planes[1]], im[planes[1]], INVERSE_LOW)
            for i in range(2):
                out[pl.ds(2 * (p + i) + r, CHIPS, stride=8), :] = words[i]


def half_planes(ref, first, tyh, tyl, txh, txl):
    sign = signs(N)
    words = [
        jnp.concatenate([ref[pl.ds(2 * p + r, CHIPS, stride=8), :] for r in range(2)], 0)
        for p in (first, first + 1)
    ]
    parts = unpack(*words, INVERSE_LOW)
    out = []
    for q in range(2):
        re, im = parts[2 * q : 2 * q + 2]
        g = jnp.concatenate([jnp.concatenate([re, im], 1), jnp.concatenate([-im, re], 1)], 0)
        out.append(right3(left3(tyh[...], tyl[...], g) * sign, txh, txl))
    return out


def own_kernel(core_ref, own, tyh, tyl, txh, txl, out):
    core = core_ref[0]
    for q, term in enumerate(half_planes(own, 0, tyh, tyl, txh[core], txl[core])):
        out[q] = term


def update_kernel(core_ref, partial, other, rho_ref, support, tyh, tyl, txh, txl, out):
    core = 1 - core_ref[0]
    for q, term in enumerate(half_planes(other, 2, tyh, tyl, txh[core], txl[core])):
        moduled = partial[q] + term
        rho = rho_ref[q].astype(jnp.float32)
        mask = support[q].astype(jnp.float32)
        out[q] = (rho + mask * (2.0 * moduled - rho) - moduled).astype(jnp.bfloat16)


SMEM = pl.BlockSpec(memory_space=pltpu.SMEM)
VMEM = pl.BlockSpec(memory_space=pltpu.VMEM)
HBM = pl.BlockSpec(memory_space=pltpu.HBM)


def call(kernel, out_shape, operands, in_specs, flops, vmem=40 * 2**20, **more):
    return pl.pallas_call(
        kernel,
        out_shape=out_shape,
        in_specs=in_specs,
        out_specs=jax.tree.map(lambda _: VMEM, out_shape),
        compiler_params=pltpu.CompilerParams(vmem_limit_bytes=vmem),
        cost_estimate=pl.CostEstimate(
            flops=int(flops), bytes_accessed=2 * 2**20, transcendentals=0
        ),
        **more,
    )(*operands)


def shards(density, amplitudes, support):
    c = {k: jax.tree.map(jnp.asarray, v) for k, v in constants().items()}
    swap = [(i, i ^ 1) for i in range(2 * CHIPS)]
    same_core = [[int(2 * chip + core) for chip in ORDER] for core in range(2)]
    core = (lax.axis_index("slab") % 2).astype(jnp.int32).reshape(1)

    def exchange(x):
        return lax.all_to_all(
            x, "slab", split_axis=0, concat_axis=0, tiled=True, axis_index_groups=same_core
        )

    def shape(dims, kind):
        return jax.ShapeDtypeStruct(dims, kind)

    density_other = lax.ppermute(density, "slab", swap)
    amplitudes_other = lax.ppermute(amplitudes, "slab", swap)
    table = lax.dynamic_index_in_dim(c["first"], core[0], 0, keepdims=False)
    own = jnp.concatenate([density, amplitudes], 0)
    sent = call(
        forward_kernel,
        shape((CHIPS * 16, HALF), jnp.int32),
        (own, density_other, amplitudes_other, table),
        [VMEM] * 4,
        800e6,
    )
    lines = exchange(sent.reshape(CHIPS, 16, HALF)).reshape(CHIPS * 16, HALF)
    sent = call(
        middle_kernel,
        shape((CHIPS * 8, HALF), jnp.int32),
        (core, lines, *c["tz"], *c["tzi"], c["rev_all"]),
        [SMEM] + [VMEM] * 6,
        800e6,
    )
    planes = exchange(sent.reshape(CHIPS, 8, HALF)).reshape(CHIPS * 8, HALF)
    planes_other = lax.ppermute(planes, "slab", swap)
    tables = (*c["tyi"], *c["txi"])
    partial = call(
        own_kernel,
        shape(density.shape, jnp.float32),
        (core, planes, *tables),
        [SMEM] + [VMEM] * 5,
        400e6,
    )
    return call(
        update_kernel,
        shape(density.shape, jnp.bfloat16),
        (core, partial, planes_other, density, support, *tables),
        [SMEM] + [VMEM] * 8,
        400e6,
    )


def solution(mesh):
    spec = P("slab", "member", None)
    return jax.shard_map(
        shards, mesh=mesh, in_specs=(spec, spec, spec), out_specs=spec, check_vma=False
    )
```

```python
import functools

import jax
import jax.numpy as jnp
import ml_dtypes
import numpy as np
from jax import lax
from jax.experimental import pallas as pl
from jax.experimental.pallas import tpu as pltpu
from jax.sharding import PartitionSpec as P

N = 256
CHIPS = 64
HALF = N // 2
QUARTER = N // 4
FLOOR = 0.25
FULL = 16380.0
FORWARD_LOW = -20
INVERSE_LOW = -25
AMP_UNIT = 512.0
ORDER = np.arange(CHIPS) ^ 44


def angles(k, position):
    turns = np.outer(2 * np.asarray(k) - (N - 1), np.asarray(position)) % (2 * N)
    return turns * (np.pi / N)


def split(table):
    high = table.astype(ml_dtypes.bfloat16)
    low = (table - high.astype(np.float64)).astype(ml_dtypes.bfloat16)
    return high, low


def two(tables):
    highs, lows = zip(*(split(t) for t in tables))
    return np.stack(highs), np.stack(lows)


def turned(c, s):
    return np.concatenate([np.concatenate([c, -s], 1), np.concatenate([s, c], 1)], 0)


@functools.cache
def constants():
    out = {}
    scale = 1.0 / np.sqrt(N)
    every = np.arange(N)
    half = np.arange(HALF)
    a = angles(half, 2 * half)
    ty = turned(np.cos(a), -np.sin(a)) * scale
    out["tyi"] = split(turned(np.cos(a.T), np.sin(a.T)) * scale)
    lanes = np.repeat([0, 1], QUARTER)
    a = angles(half, lanes)
    out["tw"] = np.stack([np.cos(a), np.sin(a)]).astype(np.float32)
    first, inverse = [], []
    rev = np.zeros((HALF, N))
    rev[:, :HALF] = np.eye(HALF)[::-1]
    for core in range(2):
        kx = np.arange(QUARTER) + QUARTER * core
        a = angles(kx, every)
        tx = np.concatenate([np.cos(a), -np.sin(a)], 0)
        inverse.append(tx * (2.0 * scale))
        pick = np.zeros((N, N))
        for h in range(2):
            pick[kx, QUARTER * h + np.arange(QUARTER)] = 1
            pick[N - 1 - kx, HALF + QUARTER * h + np.arange(QUARTER)] = 1
        parts = [np.concatenate(split(tx.T * scale), 1), *split(ty), pick, rev]
        first.append(np.concatenate([p.astype(ml_dtypes.bfloat16) for p in parts], 0))
    out["first"] = np.stack(first)
    out["txi"] = two(inverse)
    forward, inverse, twist = [], [], []
    for core in range(2):
        planes = [0, 1, 2, 3] if core == 0 else [2, 3, 0, 1]
        kz = np.concatenate([4 * ORDER[CHIPS // 2 :] + p for p in planes])
        z = np.concatenate([4 * ORDER + p for p in planes[::2]])
        a = angles(kz, z)
        forward.append(turned(np.cos(a), -np.sin(a)) * scale)
        inverse.append(turned(np.cos(a.T), np.sin(a.T)) * scale)
        a = angles(kz, np.ones(HALF, int))
        twist.append(np.stack([np.cos(a), np.sin(a)]))
        kz = np.concatenate([kz, kz + HALF])
        out["rev_all"] = (kz[:, None] + kz[None, :] == N - 1).astype(ml_dtypes.bfloat16)
    out["tz"] = two(forward)
    out["tzi"] = two(inverse)
    out["tzw"] = np.stack(twist).astype(np.float32)
    return out


def mm(a, b):
    return jnp.dot(a, b, preferred_element_type=jnp.float32)


def cut(x):
    high = x.astype(jnp.bfloat16)
    return high, (x - high.astype(jnp.float32)).astype(jnp.bfloat16)


def left3(high, low, x):
    xh, xl = cut(x)
    return mm(high, xh) + (mm(high, xl) + mm(low, xh))


def pack(re0, im0, re1, im1, low):
    m = jnp.maximum(jnp.maximum(jnp.abs(re0), jnp.abs(im0)), jnp.maximum(jnp.abs(re1), jnp.abs(im1)))
    e = jnp.clip(jnp.floor(jnp.log2(jnp.maximum(m, 1e-30))) + (1.0 - low), 0.0, 31.0)
    s = jnp.exp2(-(e + low)) * FULL
    e = e.astype(jnp.int32)

    def code(x, factor):
        return jnp.floor(x * factor + 0.5).astype(jnp.int32)

    word0 = (code(re0, s) << 17) | ((code(im0, s) & 0x7FFF) << 2) | (e & 3)
    word1 = (code(re1, s) << 17) | ((code(im1, 0.5 * s) & 0x3FFF) << 3) | (e >> 2)
    return word0, word1


def unpack(word0, word1, low):
    e = (word0 & 3) | ((word1 & 7) << 2)
    s = jnp.exp2(e.astype(jnp.float32) + low) * (1.0 / FULL)
    re0 = (word0 >> 17).astype(jnp.float32) * s
    im0 = ((word0 << 15) >> 17).astype(jnp.float32) * s
    re1 = (word1 >> 17).astype(jnp.float32) * s
    im1 = ((word1 << 15) >> 18).astype(jnp.float32) * (2.0 * s)
    return re0, im0, re1, im1


def roll(x):
    return pltpu.roll(x, QUARTER, 1)


def lower(rows):
    return lax.broadcasted_iota(jnp.int32, (rows, HALF), 1) < QUARTER


def butterfly(x, low):
    return roll(x) + jnp.where(low, x, -x)


def square(x):
    return jnp.concatenate(
        [jnp.concatenate([x[0], x[2]], 1), jnp.concatenate([x[1], x[3]], 1)], 0
    )


def forward_planes(first, rho_ref, amp_ref, table, tw, out, scratch):
    low = lower(HALF)
    c, s = tw[0], tw[1]
    stack = []
    for q in range(2):
        a = mm(rho_ref[q], table[:N])
        scratch[q] = a[:, :HALF] + a[:, HALF:]
        even = scratch[q, pl.ds(0, HALF, stride=2), :]
        odd = scratch[q, pl.ds(1, HALF, stride=2), :]
        stack += [jnp.where(low, even, roll(odd)), jnp.where(low, roll(even), odd)]
    u = left3(table[N : 2 * N], table[2 * N : 3 * N], square(stack))
    parts = []
    for q in range(2):
        re, im = u[:HALF, HALF * q : HALF * (q + 1)], u[HALF:, HALF * q : HALF * (q + 1)]
        parts += [butterfly(re * c + im * s, low), butterfly(im * c - re * s, low)]
    words = pack(*parts, FORWARD_LOW)
    mirrors = []
    directs = []
    for q in range(2):
        both = mm(amp_ref[q], table[3 * N : 4 * N])
        directs.append(jnp.where(low, both[:HALF, :HALF], both[HALF:, :HALF]))
        mirrors.append(jnp.where(low, both[HALF:, HALF:], both[:HALF, HALF:]))
    mirrors = mm(table[4 * N :, :HALF], jnp.concatenate(mirrors, 1).astype(jnp.bfloat16))
    for q in range(2):
        mirror = mirrors[:, HALF * q : HALF * (q + 1)]
        coded = ((directs[q] * AMP_UNIT).astype(jnp.int32) << 16) | (mirror * AMP_UNIT).astype(jnp.int32)
        for r in range(2):
            rows = slice(CHIPS * r, CHIPS * (r + 1))
            slot = 2 * (first + q) + r
            out[pl.ds(slot, CHIPS, stride=16), :] = words[q][rows]
            out[pl.ds(8 + slot, CHIPS, stride=16), :] = coded[rows]


def forward_kernel(rho, amp, rho_other, amp_other, table, tw, out, scratch):
    forward_planes(0, rho, amp, table, tw, out, scratch.at[:2])
    forward_planes(2, rho_other, amp_other, table, tw, out, scratch.at[2:])


def middle_kernel(core_ref, msg, tzh, tzl, tzih, tzil, tzw, rev, out):
    core = core_ref[0]
    c, s = tzw[core, 0], tzw[core, 1]
    half = CHIPS // 2
    spectra, mirrors, directs = [], [], []
    for r in range(2):
        parts = []
        for p in (0, 2):
            pair = [msg[pl.ds(2 * (p + i) + r, CHIPS, stride=16), :] for i in range(2)]
            parts.append(unpack(*pair, FORWARD_LOW))
        lines = square([jnp.concatenate(x, 0) for x in zip(*parts)])
        u = left3(tzh[core], tzl[core], lines)
        even_re, odd_re = u[:HALF, :HALF], u[:HALF, HALF:]
        even_im, odd_im = u[HALF:, :HALF], u[HALF:, HALF:]
        odd_re, odd_im = odd_re * c + odd_im * s, odd_im * c - odd_re * s
        spectra.append(
            (
                jnp.concatenate([even_re + odd_re, even_re - odd_re], 0),
                jnp.concatenate([even_im + odd_im, even_im - odd_im], 0),
            )
        )
        coded = jnp.concatenate(
            [
                msg[pl.ds(16 * chip + 8 + 2 * p + r, half, stride=16), :]
                for chip in (half, 0)
                for p in range(4)
            ],
            0,
        )
        directs.append((coded >> 16).astype(jnp.float32))
        mirrors.append((coded & 0xFFFF).astype(jnp.float32).astype(jnp.bfloat16))
    mirrors = mm(rev[...], jnp.concatenate(mirrors, 1))
    for r in range(2):
        re, im = spectra[r]
        target = (directs[r] + mirrors[:, HALF * r : HALF * (r + 1)]) * (0.5 / AMP_UNIT)
        ratio = target / jnp.maximum(jnp.sqrt(re * re + im * im), FLOOR)
        re, im = re * ratio, im * ratio
        odd_re, odd_im = re[:HALF] - re[HALF:], im[:HALF] - im[HALF:]
        lines = square(
            [
                re[:HALF] + re[HALF:],
                im[:HALF] + im[HALF:],
                odd_re * c - odd_im * s,
                odd_im * c + odd_re * s,
            ]
        )
        u = left3(tzih[core], tzil[core], lines)
        for i in range(2):
            re, im = u[CHIPS * i : CHIPS * (i + 1)], u[HALF + CHIPS * i : HALF + CHIPS * (i + 1)]
            words = pack(re[:, :HALF], im[:, :HALF], re[:, HALF:], im[:, HALF:], INVERSE_LOW)
            for o in range(2):
                out[pl.ds(2 * (2 * i + o) + r, CHIPS, stride=8), :] = words[o]


def half_planes(ref, first, tyh, tyl, tw, txh, txl):
    low = lower(HALF)
    c, s = tw[0], tw[1]
    words = [
        jnp.concatenate([ref[pl.ds(2 * p + r, CHIPS, stride=8), :] for r in range(2)], 0)
        for p in (first, first + 1)
    ]
    parts = unpack(*words, INVERSE_LOW)
    stack = []
    for q in range(2):
        re, im = (butterfly(x, low) for x in parts[2 * q : 2 * q + 2])
        stack += [re * c - im * s, im * c + re * s]
    u = left3(tyh[...], tyl[...], square(stack))
    out = []
    for q in range(2):
        re, im = u[:HALF, HALF * q : HALF * (q + 1)], u[HALF:, HALF * q : HALF * (q + 1)]
        lines = jnp.concatenate(
            [jnp.where(low, re, roll(im)), jnp.where(low, roll(re), im)], 0
        )
        lh, ll = cut(lines)
        out.append(
            mm(jnp.concatenate([lh, ll], 1), jnp.concatenate([txh, txh], 0)) + mm(lh, txl)
        )
    return out


def own_kernel(core_ref, own, tyh, tyl, tw, txh, txl, out):
    core = core_ref[0]
    for q, term in enumerate(half_planes(own, 0, tyh, tyl, tw, txh[core], txl[core])):
        out[q] = term


def update_kernel(core_ref, partial, other, rho_ref, support, tyh, tyl, tw, txh, txl, out, scratch):
    core = 1 - core_ref[0]
    for q, term in enumerate(half_planes(other, 2, tyh, tyl, tw, txh[core], txl[core])):
        moduled = partial[q] + term
        for side in range(2):
            lanes = slice(HALF * side, HALF * (side + 1))
            for o in range(2):
                rows = moduled[HALF * o : HALF * (o + 1), lanes]
                scratch[2 * q + side, pl.ds(o, HALF, stride=2), :] = rows
            rho = rho_ref[q, :, lanes].astype(jnp.float32)
            mask = support[q, :, lanes].astype(jnp.float32)
            m = scratch[2 * q + side]
            out[q, :, lanes] = (rho + mask * (2.0 * m - rho) - m).astype(jnp.bfloat16)


SMEM = pl.BlockSpec(memory_space=pltpu.SMEM)
VMEM = pl.BlockSpec(memory_space=pltpu.VMEM)
HBM = pl.BlockSpec(memory_space=pltpu.HBM)


def call(kernel, out_shape, operands, in_specs, flops, vmem=40 * 2**20, **more):
    return pl.pallas_call(
        kernel,
        out_shape=out_shape,
        in_specs=in_specs,
        out_specs=jax.tree.map(lambda _: VMEM, out_shape),
        compiler_params=pltpu.CompilerParams(vmem_limit_bytes=vmem),
        cost_estimate=pl.CostEstimate(
            flops=int(flops), bytes_accessed=2 * 2**20, transcendentals=0
        ),
        **more,
    )(*operands)


def shards(density, amplitudes, support):
    c = {k: jax.tree.map(jnp.asarray, v) for k, v in constants().items()}
    swap = [(i, i ^ 1) for i in range(2 * CHIPS)]
    same_core = [[int(2 * chip + core) for chip in ORDER] for core in range(2)]
    core = (lax.axis_index("slab") % 2).astype(jnp.int32).reshape(1)

    def exchange(x):
        return lax.all_to_all(
            x, "slab", split_axis=0, concat_axis=0, tiled=True, axis_index_groups=same_core
        )

    def shape(dims, kind):
        return jax.ShapeDtypeStruct(dims, kind)

    density_other = lax.ppermute(density, "slab", swap)
    amplitudes_other = lax.ppermute(amplitudes, "slab", swap)
    table = lax.dynamic_index_in_dim(c["first"], core[0], 0, keepdims=False)
    sent = call(
        forward_kernel,
        shape((CHIPS * 16, HALF), jnp.int32),
        (density, amplitudes, density_other, amplitudes_other, table, c["tw"]),
        [VMEM] * 6,
        800e6,
        scratch_shapes=[pltpu.VMEM((4, N, HALF), jnp.float32)],
    )
    lines = exchange(sent.reshape(CHIPS, 16, HALF)).reshape(CHIPS * 16, HALF)
    sent = call(
        middle_kernel,
        shape((CHIPS * 8, HALF), jnp.int32),
        (core, lines, *c["tz"], *c["tzi"], c["tzw"], c["rev_all"]),
        [SMEM] + [VMEM] * 7,
        800e6,
    )
    planes = exchange(sent.reshape(CHIPS, 8, HALF)).reshape(CHIPS * 8, HALF)
    planes_other = lax.ppermute(planes, "slab", swap)
    tables = (*c["tyi"], c["tw"], *c["txi"])
    partial = call(
        own_kernel,
        shape(density.shape, jnp.float32),
        (core, planes, *tables),
        [SMEM] + [VMEM] * 6,
        400e6,
    )
    return call(
        update_kernel,
        shape(density.shape, jnp.bfloat16),
        (core, partial, planes_other, density, support, *tables),
        [SMEM] + [VMEM] * 9,
        400e6,
        scratch_shapes=[pltpu.VMEM((4, N, HALF), jnp.float32)],
    )


def solution(mesh):
    spec = P("slab", "member", None)
    return jax.shard_map(
        shards, mesh=mesh, in_specs=(spec, spec, spec), out_specs=spec, check_vma=False
    )
```

```python
import functools

import jax
import jax.numpy as jnp
import ml_dtypes
import numpy as np
from jax import lax
from jax.experimental import pallas as pl
from jax.experimental.pallas import tpu as pltpu
from jax.sharding import PartitionSpec as P

N = 256
CHIPS = 64
HALF = N // 2
QUARTER = N // 4
FLOOR = 0.25
FULL = 16380.0
FORWARD_LOW = -20
INVERSE_LOW = -25
AMP_UNIT = 512.0
ORDER = np.arange(CHIPS) ^ 44


def angles(k, position):
    turns = np.outer(2 * np.asarray(k) - (N - 1), np.asarray(position)) % (2 * N)
    return turns * (np.pi / N)


def split(table):
    high = table.astype(ml_dtypes.bfloat16)
    low = (table - high.astype(np.float64)).astype(ml_dtypes.bfloat16)
    return high, low


def two(tables):
    highs, lows = zip(*(split(t) for t in tables))
    return np.stack(highs), np.stack(lows)


def turned(c, s):
    return np.concatenate([np.concatenate([c, -s], 1), np.concatenate([s, c], 1)], 0)


@functools.cache
def constants():
    out = {}
    scale = 1.0 / np.sqrt(N)
    every = np.arange(N)
    half = np.arange(HALF)
    a = angles(half, 2 * half)
    ty = turned(np.cos(a), -np.sin(a)) * scale
    out["tyi"] = split(turned(np.cos(a.T), np.sin(a.T)) * scale)
    lanes = np.repeat([0, 1], QUARTER)
    a = angles(half, lanes)
    out["tw"] = np.stack([np.cos(a), np.sin(a)]).astype(np.float32)
    first, inverse = [], []
    rev = np.zeros((HALF, N))
    rev[:, :HALF] = np.eye(HALF)[::-1]
    for core in range(2):
        kx = np.arange(QUARTER) + QUARTER * core
        a = angles(kx, every)
        tx = np.concatenate([np.cos(a), -np.sin(a)], 0)
        inverse.append(tx * (2.0 * scale))
        pick = np.zeros((N, N))
        for h in range(2):
            pick[kx, QUARTER * h + np.arange(QUARTER)] = 1
            pick[N - 1 - kx, HALF + QUARTER * h + np.arange(QUARTER)] = 1
        parts = [np.concatenate(split(tx.T * scale), 1), *split(ty), pick, rev]
        first.append(np.concatenate([p.astype(ml_dtypes.bfloat16) for p in parts], 0))
    out["first"] = np.stack(first)
    out["txi"] = two(inverse)
    forward, inverse, twist = [], [], []
    for core in range(2):
        planes = [0, 1, 2, 3] if core == 0 else [2, 3, 0, 1]
        kz = np.concatenate([4 * ORDER[CHIPS // 2 :] + p for p in planes])
        z = np.concatenate([4 * ORDER + p for p in planes[::2]])
        a = angles(kz, z)
        forward.append(turned(np.cos(a), -np.sin(a)) * scale)
        inverse.append(turned(np.cos(a.T), np.sin(a.T)) * scale)
        a = angles(kz, np.ones(HALF, int))
        twist.append(np.stack([np.cos(a), np.sin(a)]))
        kz = np.concatenate([kz, kz + HALF])
        out["rev_all"] = (kz[:, None] + kz[None, :] == N - 1).astype(ml_dtypes.bfloat16)
    out["tz"] = two(forward)
    out["tzi"] = two(inverse)
    out["tzw"] = np.stack(twist).astype(np.float32)
    return out


def mm(a, b):
    return jnp.dot(a, b, preferred_element_type=jnp.float32)


def cut(x):
    high = x.astype(jnp.bfloat16)
    return high, (x - high.astype(jnp.float32)).astype(jnp.bfloat16)


def left3(high, low, x):
    xh, xl = cut(x)
    return mm(high, xh) + (mm(high, xl) + mm(low, xh))


def pack(re0, im0, re1, im1, low):
    m = jnp.maximum(jnp.maximum(jnp.abs(re0), jnp.abs(im0)), jnp.maximum(jnp.abs(re1), jnp.abs(im1)))
    e = jnp.clip(jnp.floor(jnp.log2(jnp.maximum(m, 1e-30))) + (1.0 - low), 0.0, 31.0)
    s = jnp.exp2(-(e + low)) * FULL
    e = e.astype(jnp.int32)

    def code(x, factor, middle):
        return (x * factor + (middle + 0.5)).astype(jnp.int32)

    word0 = (code(re0, s, 16384) << 17) | (code(im0, s, 16384) << 2) | (e & 3)
    word1 = (code(re1, s, 16384) << 17) | (code(im1, 0.5 * s, 8192) << 3) | (e >> 2)
    return word0, word1


def unpack(word0, word1, low):
    e = (word0 & 3) | ((word1 & 7) << 2)
    s = jnp.exp2(e.astype(jnp.float32) + low) * (1.0 / FULL)

    def value(code, factor, middle):
        return (code - middle).astype(jnp.float32) * factor

    re0 = value(lax.shift_right_logical(word0, 17), s, 16384)
    im0 = value((word0 >> 2) & 0x7FFF, s, 16384)
    re1 = value(lax.shift_right_logical(word1, 17), s, 16384)
    im1 = value((word1 >> 3) & 0x3FFF, 2.0 * s, 8192)
    return re0, im0, re1, im1


def roll(x):
    return pltpu.roll(x, QUARTER, 1)


def lower(rows):
    return lax.broadcasted_iota(jnp.int32, (rows, HALF), 1) < QUARTER


def butterfly(x, low):
    return roll(x) + jnp.where(low, x, -x)


def square(x):
    return jnp.concatenate(
        [jnp.concatenate([x[0], x[2]], 1), jnp.concatenate([x[1], x[3]], 1)], 0
    )


def forward_kernel(rho_own, amp_own, rho_other, amp_other, table, tw, out, scratch):
    low = lower(HALF)
    c, s = tw[0], tw[1]
    rho = [rho_own[0], rho_own[1], rho_other[0], rho_other[1]]
    amp = [amp_own[0], amp_own[1], amp_other[0], amp_other[1]]

    def along_x(p):
        a = mm(rho[p], table[:N])
        scratch[p] = a[:, :HALF] + a[:, HALF:]
        even = scratch[p, pl.ds(0, HALF, stride=2), :]
        odd = scratch[p, pl.ds(1, HALF, stride=2), :]
        return [jnp.where(low, even, roll(odd)), jnp.where(low, roll(even), odd)]

    def along_y(stack):
        u = left3(table[N : 2 * N], table[2 * N : 3 * N], square(stack))
        parts = []
        for q in range(2):
            re, im = u[:HALF, HALF * q : HALF * (q + 1)], u[HALF:, HALF * q : HALF * (q + 1)]
            parts += [butterfly(re * c + im * s, low), butterfly(im * c - re * s, low)]
        return parts

    def picked(p):
        both = mm(amp[p], table[3 * N : 4 * N])
        direct = jnp.where(low, both[:HALF, :HALF], both[HALF:, :HALF])
        return direct, jnp.where(low, both[HALF:, HALF:], both[:HALF, HALF:])

    def store(slot, words):
        for r in range(2):
            out[pl.ds(slot + r, CHIPS, stride=16), :] = words[CHIPS * r : CHIPS * (r + 1)]

    lines = [along_x(p) for p in range(4)]
    first = along_y(lines[0] + lines[1])
    directs, mirrors = zip(*(picked(p) for p in range(4)))
    second = along_y(lines[2] + lines[3])
    for q, words in enumerate(pack(*first, FORWARD_LOW)):
        store(2 * q, words)
    mirrors = mm(table[4 * N :, :HALF], jnp.concatenate(mirrors, 1).astype(jnp.bfloat16))
    for p in range(4):
        mirror = (mirrors[:, HALF * p : HALF * (p + 1)] * AMP_UNIT).astype(jnp.int32)
        store(8 + 2 * p, ((directs[p] * AMP_UNIT).astype(jnp.int32) << 16) | mirror)
    for q, words in enumerate(pack(*second, FORWARD_LOW)):
        store(4 + 2 * q, words)


def middle_kernel(core_ref, msg, tzh, tzl, tzih, tzil, tzw, rev, out):
    core = core_ref[0]
    c, s = tzw[core, 0], tzw[core, 1]
    half = CHIPS // 2
    spectra, mirrors, directs = [], [], []
    for r in range(2):
        parts = []
        for p in (0, 2):
            pair = [msg[pl.ds(2 * (p + i) + r, CHIPS, stride=16), :] for i in range(2)]
            parts.append(unpack(*pair, FORWARD_LOW))
        lines = square([jnp.concatenate(x, 0) for x in zip(*parts)])
        u = left3(tzh[core], tzl[core], lines)
        even_re, odd_re = u[:HALF, :HALF], u[:HALF, HALF:]
        even_im, odd_im = u[HALF:, :HALF], u[HALF:, HALF:]
        odd_re, odd_im = odd_re * c + odd_im * s, odd_im * c - odd_re * s
        spectra.append(
            (
                jnp.concatenate([even_re + odd_re, even_re - odd_re], 0),
                jnp.concatenate([even_im + odd_im, even_im - odd_im], 0),
            )
        )
        coded = jnp.concatenate(
            [
                msg[pl.ds(16 * chip + 8 + 2 * p + r, half, stride=16), :]
                for chip in (half, 0)
                for p in range(4)
            ],
            0,
        )
        directs.append((coded >> 16).astype(jnp.float32))
        mirrors.append((coded & 0xFFFF).astype(jnp.float32).astype(jnp.bfloat16))
    mirrors = mm(rev[...], jnp.concatenate(mirrors, 1))
    for r in range(2):
        re, im = spectra[r]
        target = (directs[r] + mirrors[:, HALF * r : HALF * (r + 1)]) * (0.5 / AMP_UNIT)
        ratio = target * lax.rsqrt(jnp.maximum(re * re + im * im, FLOOR * FLOOR))
        re, im = re * ratio, im * ratio
        odd_re, odd_im = re[:HALF] - re[HALF:], im[:HALF] - im[HALF:]
        lines = square(
            [
                re[:HALF] + re[HALF:],
                im[:HALF] + im[HALF:],
                odd_re * c - odd_im * s,
                odd_im * c + odd_re * s,
            ]
        )
        u = left3(tzih[core], tzil[core], lines)
        for i in range(2):
            re, im = u[CHIPS * i : CHIPS * (i + 1)], u[HALF + CHIPS * i : HALF + CHIPS * (i + 1)]
            words = pack(re[:, :HALF], im[:, :HALF], re[:, HALF:], im[:, HALF:], INVERSE_LOW)
            for o in range(2):
                out[pl.ds(2 * (2 * i + o) + r, CHIPS, stride=8), :] = words[o]


def half_planes(ref, first, tyh, tyl, tw, txh, txl):
    low = lower(HALF)
    c, s = tw[0], tw[1]
    words = [
        jnp.concatenate([ref[pl.ds(2 * p + r, CHIPS, stride=8), :] for r in range(2)], 0)
        for p in (first, first + 1)
    ]
    parts = unpack(*words, INVERSE_LOW)
    stack = []
    for q in range(2):
        re, im = (butterfly(x, low) for x in parts[2 * q : 2 * q + 2])
        stack += [re * c - im * s, im * c + re * s]
    u = left3(tyh[...], tyl[...], square(stack))
    out = []
    for q in range(2):
        re, im = u[:HALF, HALF * q : HALF * (q + 1)], u[HALF:, HALF * q : HALF * (q + 1)]
        lines = jnp.concatenate(
            [jnp.where(low, re, roll(im)), jnp.where(low, roll(re), im)], 0
        )
        lh, ll = cut(lines)
        out.append(
            mm(jnp.concatenate([lh, ll], 1), jnp.concatenate([txh, txh], 0)) + mm(lh, txl)
        )
    return out


def interleave(rows, side, scratch):
    for o in range(2):
        scratch[pl.ds(o, HALF, stride=2), :] = rows[
            HALF * o : HALF * (o + 1), HALF * side : HALF * (side + 1)
        ]
    return scratch[...]


def own_kernel(core_ref, own, rho_ref, support, tyh, tyl, tw, txh, txl, out, scratch):
    core = core_ref[0]
    for q, term in enumerate(half_planes(own, 0, tyh, tyl, tw, txh[core], txl[core])):
        for side in range(2):
            lanes = slice(HALF * side, HALF * (side + 1))
            m = interleave(term, side, scratch.at[2 * q + side])
            rho = rho_ref[q, :, lanes].astype(jnp.float32)
            mask = support[q, :, lanes].astype(jnp.float32)
            out[q, :, lanes] = rho + mask * (2.0 * m - rho) - m


def update_kernel(core_ref, partial, other, support, tyh, tyl, tw, txh, txl, out, scratch, done, sems):
    core = 1 - core_ref[0]
    copies = []
    for q, term in enumerate(half_planes(other, 2, tyh, tyl, tw, txh[core], txl[core])):
        for side in range(2):
            lanes = slice(HALF * side, HALF * (side + 1))
            m = interleave(term, side, scratch.at[2 * q + side])
            mask = support[q, :, lanes].astype(jnp.float32)
            done[q, :, lanes] = (partial[q, :, lanes] + (2.0 * mask - 1.0) * m).astype(jnp.bfloat16)
        copies.append(pltpu.make_async_copy(done.at[q], out.at[q], sems.at[q]))
        copies[q].start()
    for copy in copies:
        copy.wait()


SMEM = pl.BlockSpec(memory_space=pltpu.SMEM)
VMEM = pl.BlockSpec(memory_space=pltpu.VMEM)
HBM = pl.BlockSpec(memory_space=pltpu.HBM)


def call(kernel, out_shape, operands, in_specs, flops, out_specs=VMEM, **more):
    return pl.pallas_call(
        kernel,
        out_shape=out_shape,
        in_specs=in_specs,
        out_specs=out_specs,
        compiler_params=pltpu.CompilerParams(vmem_limit_bytes=40 * 2**20),
        cost_estimate=pl.CostEstimate(
            flops=int(flops), bytes_accessed=2 * 2**20, transcendentals=0
        ),
        **more,
    )(*operands)


def shards(density, amplitudes, support):
    c = {k: jax.tree.map(jnp.asarray, v) for k, v in constants().items()}
    swap = [(i, i ^ 1) for i in range(2 * CHIPS)]
    same_core = [[int(2 * chip + core) for chip in ORDER] for core in range(2)]
    core = (lax.axis_index("slab") % 2).astype(jnp.int32).reshape(1)

    def exchange(x):
        return lax.all_to_all(
            x, "slab", split_axis=0, concat_axis=0, tiled=True, axis_index_groups=same_core
        )

    def shape(dims, kind):
        return jax.ShapeDtypeStruct(dims, kind)

    density_other = lax.ppermute(density, "slab", swap)
    amplitudes_other = lax.ppermute(amplitudes, "slab", swap)
    table = lax.dynamic_index_in_dim(c["first"], core[0], 0, keepdims=False)
    sent = call(
        forward_kernel,
        shape((CHIPS * 16, HALF), jnp.int32),
        (density, amplitudes, density_other, amplitudes_other, table, c["tw"]),
        [VMEM] * 6,
        800e6,
        scratch_shapes=[pltpu.VMEM((4, N, HALF), jnp.float32)],
    )
    lines = exchange(sent.reshape(CHIPS, 16, HALF)).reshape(CHIPS * 16, HALF)
    sent = call(
        middle_kernel,
        shape((CHIPS * 8, HALF), jnp.int32),
        (core, lines, *c["tz"], *c["tzi"], c["tzw"], c["rev_all"]),
        [SMEM] + [VMEM] * 7,
        800e6,
    )
    planes = exchange(sent.reshape(CHIPS, 8, HALF)).reshape(CHIPS * 8, HALF)
    planes_other = lax.ppermute(planes, "slab", swap)
    tables = (*c["tyi"], c["tw"], *c["txi"])
    partial = call(
        own_kernel,
        shape(density.shape, jnp.float32),
        (core, planes, density, support, *tables),
        [SMEM] + [VMEM] * 8,
        400e6,
        scratch_shapes=[pltpu.VMEM((4, N, HALF), jnp.float32)],
    )
    return call(
        update_kernel,
        shape(density.shape, jnp.bfloat16),
        (core, partial, planes_other, support, *tables),
        [SMEM] + [VMEM] * 8,
        400e6,
        out_specs=HBM,
        scratch_shapes=[
            pltpu.VMEM((4, N, HALF), jnp.float32),
            pltpu.VMEM(density.shape, jnp.bfloat16),
            pltpu.SemaphoreType.DMA((2,)),
        ],
    )


def solution(mesh):
    spec = P("slab", "member", None)
    return jax.shard_map(
        shards, mesh=mesh, in_specs=(spec, spec, spec), out_specs=spec, check_vma=False
    )
```

```python
import functools

import jax
import jax.numpy as jnp
import ml_dtypes
import numpy as np
from jax import lax
from jax.experimental import pallas as pl
from jax.experimental.pallas import tpu as pltpu
from jax.sharding import PartitionSpec as P

N = 256
CHIPS = 64
HALF = N // 2
QUARTER = N // 4
FLOOR = 0.25
FULL = 16380.0
FORWARD_LOW = -20
INVERSE_LOW = -25
AMP_UNIT = 512.0
ORDER = np.arange(CHIPS) ^ 44


def angles(k, position):
    turns = np.outer(2 * np.asarray(k) - (N - 1), np.asarray(position)) % (2 * N)
    return turns * (np.pi / N)


def split(table):
    high = table.astype(ml_dtypes.bfloat16)
    low = (table - high.astype(np.float64)).astype(ml_dtypes.bfloat16)
    return high, low


def two(tables):
    highs, lows = zip(*(split(t) for t in tables))
    return np.stack(highs), np.stack(lows)


def turned(c, s):
    return np.concatenate([np.concatenate([c, -s], 1), np.concatenate([s, c], 1)], 0)


@functools.cache
def constants():
    out = {}
    scale = 1.0 / np.sqrt(N)
    every = np.arange(N)
    half = np.arange(HALF)
    a = angles(half, 2 * half)
    ty = turned(np.cos(a), -np.sin(a)) * scale
    out["tyi"] = split(turned(np.cos(a.T), np.sin(a.T)) * scale)
    lanes = np.repeat([0, 1], QUARTER)
    a = angles(half, lanes)
    out["tw"] = np.stack([np.cos(a), np.sin(a)]).astype(np.float32)
    first, inverse = [], []
    rev = np.zeros((HALF, N))
    rev[:, :HALF] = np.eye(HALF)[::-1]
    for core in range(2):
        kx = np.arange(QUARTER) + QUARTER * core
        a = angles(kx, every)
        tx = np.concatenate([np.cos(a), -np.sin(a)], 0)
        inverse.append(tx * (2.0 * scale))
        pick = np.zeros((N, N))
        for h in range(2):
            pick[kx, QUARTER * h + np.arange(QUARTER)] = 1
            pick[N - 1 - kx, HALF + QUARTER * h + np.arange(QUARTER)] = 1
        parts = [np.concatenate(split(tx.T * scale), 1), *split(ty), pick, rev]
        first.append(np.concatenate([p.astype(ml_dtypes.bfloat16) for p in parts], 0))
    out["first"] = np.stack(first)
    out["txi"] = two(inverse)
    forward, inverse, twist = [], [], []
    for core in range(2):
        planes = [0, 1, 2, 3] if core == 0 else [2, 3, 0, 1]
        kz = np.concatenate([4 * ORDER[CHIPS // 2 :] + p for p in planes])
        z = np.concatenate([4 * ORDER + p for p in planes[::2]])
        a = angles(kz, z)
        forward.append(turned(np.cos(a), -np.sin(a)) * scale)
        inverse.append(turned(np.cos(a.T), np.sin(a.T)) * scale)
        a = angles(kz, np.ones(HALF, int))
        twist.append(np.stack([np.cos(a), np.sin(a)]))
        kz = np.concatenate([kz, kz + HALF])
        out["rev_all"] = (kz[:, None] + kz[None, :] == N - 1).astype(ml_dtypes.bfloat16)
    out["tz"] = two(forward)
    out["tzi"] = two(inverse)
    out["tzw"] = np.stack(twist).astype(np.float32)
    return out


def mm(a, b):
    return jnp.dot(a, b, preferred_element_type=jnp.float32)


def cut(x):
    high = x.astype(jnp.bfloat16)
    return high, (x - high.astype(jnp.float32)).astype(jnp.bfloat16)


def left3(high, low, x):
    xh, xl = cut(x)
    return mm(high, xh) + (mm(high, xl) + mm(low, xh))


def pack(re0, im0, re1, im1, low):
    m = jnp.maximum(jnp.maximum(jnp.abs(re0), jnp.abs(im0)), jnp.maximum(jnp.abs(re1), jnp.abs(im1)))
    e = jnp.clip(jnp.floor(jnp.log2(jnp.maximum(m, 1e-30))) + (1.0 - low), 0.0, 31.0)
    s = jnp.exp2(-(e + low)) * FULL
    e = e.astype(jnp.int32)

    def code(x, factor, middle):
        return (x * factor + (middle + 0.5)).astype(jnp.int32)

    word0 = (code(re0, s, 16384) << 17) | (code(im0, s, 16384) << 2) | (e & 3)
    word1 = (code(re1, s, 16384) << 17) | (code(im1, 0.5 * s, 8192) << 3) | (e >> 2)
    return word0, word1


def unpack(word0, word1, low):
    e = (word0 & 3) | ((word1 & 7) << 2)
    s = jnp.exp2(e.astype(jnp.float32) + low) * (1.0 / FULL)

    def value(code, factor, middle):
        return (code - middle).astype(jnp.float32) * factor

    re0 = value(lax.shift_right_logical(word0, 17), s, 16384)
    im0 = value((word0 >> 2) & 0x7FFF, s, 16384)
    re1 = value(lax.shift_right_logical(word1, 17), s, 16384)
    im1 = value((word1 >> 3) & 0x3FFF, 2.0 * s, 8192)
    return re0, im0, re1, im1


def roll(x):
    return pltpu.roll(x, QUARTER, 1)


def lower(rows):
    return lax.broadcasted_iota(jnp.int32, (rows, HALF), 1) < QUARTER


def butterfly(x, low):
    return roll(x) + jnp.where(low, x, -x)


def square(x):
    return jnp.concatenate(
        [jnp.concatenate([x[0], x[2]], 1), jnp.concatenate([x[1], x[3]], 1)], 0
    )


def forward_kernel(rho_own, amp_own, rho_other, amp_other, table, tw, out, scratch):
    low = lower(HALF)
    c, s = tw[0], tw[1]
    rho = [rho_own[0], rho_own[1], rho_other[0], rho_other[1]]
    amp = [amp_own[0], amp_own[1], amp_other[0], amp_other[1]]

    def along_x(p):
        a = mm(rho[p], table[:N])
        scratch[p] = a[:, :HALF] + a[:, HALF:]
        even = scratch[p, pl.ds(0, HALF, stride=2), :]
        odd = scratch[p, pl.ds(1, HALF, stride=2), :]
        return [jnp.where(low, even, roll(odd)), jnp.where(low, roll(even), odd)]

    def along_y(stack):
        u = left3(table[N : 2 * N], table[2 * N : 3 * N], square(stack))
        parts = []
        for q in range(2):
            re, im = u[:HALF, HALF * q : HALF * (q + 1)], u[HALF:, HALF * q : HALF * (q + 1)]
            parts += [butterfly(re * c + im * s, low), butterfly(im * c - re * s, low)]
        return parts

    def picked(p):
        both = mm(amp[p], table[3 * N : 4 * N])
        direct = jnp.where(low, both[:HALF, :HALF], both[HALF:, :HALF])
        return direct, jnp.where(low, both[HALF:, HALF:], both[:HALF, HALF:])

    def store(slot, words):
        for r in range(2):
            out[pl.ds(slot + r, CHIPS, stride=16), :] = words[CHIPS * r : CHIPS * (r + 1)]

    lines = [along_x(p) for p in range(4)]
    first = along_y(lines[0] + lines[1])
    directs, mirrors = zip(*(picked(p) for p in range(4)))
    second = along_y(lines[2] + lines[3])
    for q, words in enumerate(pack(*first, FORWARD_LOW)):
        store(2 * q, words)
    mirrors = mm(table[4 * N :, :HALF], jnp.concatenate(mirrors, 1).astype(jnp.bfloat16))
    for p in range(4):
        mirror = (mirrors[:, HALF * p : HALF * (p + 1)] * AMP_UNIT).astype(jnp.int32)
        store(8 + 2 * p, ((directs[p] * AMP_UNIT).astype(jnp.int32) << 16) | mirror)
    for q, words in enumerate(pack(*second, FORWARD_LOW)):
        store(4 + 2 * q, words)


def middle_kernel(core_ref, msg, tzh, tzl, tzih, tzil, tzw, rev, out):
    core = core_ref[0]
    c, s = tzw[core, 0], tzw[core, 1]
    half = CHIPS // 2
    spectra, mirrors, directs = [], [], []
    for r in range(2):
        parts = []
        for p in (0, 2):
            pair = [msg[pl.ds(2 * (p + i) + r, CHIPS, stride=16), :] for i in range(2)]
            parts.append(unpack(*pair, FORWARD_LOW))
        lines = square([jnp.concatenate(x, 0) for x in zip(*parts)])
        u = left3(tzh[core], tzl[core], lines)
        even_re, odd_re = u[:HALF, :HALF], u[:HALF, HALF:]
        even_im, odd_im = u[HALF:, :HALF], u[HALF:, HALF:]
        odd_re, odd_im = odd_re * c + odd_im * s, odd_im * c - odd_re * s
        spectra.append(
            (
                jnp.concatenate([even_re + odd_re, even_re - odd_re], 0),
                jnp.concatenate([even_im + odd_im, even_im - odd_im], 0),
            )
        )
        coded = jnp.concatenate(
            [
                msg[pl.ds(16 * chip + 8 + 2 * p + r, half, stride=16), :]
                for chip in (half, 0)
                for p in range(4)
            ],
            0,
        )
        directs.append((coded >> 16).astype(jnp.float32))
        mirrors.append((coded & 0xFFFF).astype(jnp.float32).astype(jnp.bfloat16))
    mirrors = mm(rev[...], jnp.concatenate(mirrors, 1))
    for r in range(2):
        re, im = spectra[r]
        target = (directs[r] + mirrors[:, HALF * r : HALF * (r + 1)]) * (0.5 / AMP_UNIT)
        ratio = target * lax.rsqrt(jnp.maximum(re * re + im * im, FLOOR * FLOOR))
        re, im = re * ratio, im * ratio
        odd_re, odd_im = re[:HALF] - re[HALF:], im[:HALF] - im[HALF:]
        lines = square(
            [
                re[:HALF] + re[HALF:],
                im[:HALF] + im[HALF:],
                odd_re * c - odd_im * s,
                odd_im * c + odd_re * s,
            ]
        )
        u = left3(tzih[core], tzil[core], lines)
        for i in range(2):
            re, im = u[CHIPS * i : CHIPS * (i + 1)], u[HALF + CHIPS * i : HALF + CHIPS * (i + 1)]
            words = pack(re[:, :HALF], im[:, :HALF], re[:, HALF:], im[:, HALF:], INVERSE_LOW)
            for o in range(2):
                out[pl.ds(2 * (2 * i + o) + r, CHIPS, stride=8), :] = words[o]


def half_planes(ref, first, tyh, tyl, tw, txh, txl, scratch):
    low = lower(HALF)
    c, s = tw[0], tw[1]
    words = [
        jnp.concatenate([ref[pl.ds(2 * p + r, CHIPS, stride=8), :] for r in range(2)], 0)
        for p in (first, first + 1)
    ]
    parts = unpack(*words, INVERSE_LOW)
    stack = []
    for q in range(2):
        re, im = (butterfly(x, low) for x in parts[2 * q : 2 * q + 2])
        stack += [re * c - im * s, im * c + re * s]
    u = left3(tyh[...], tyl[...], square(stack))
    out = []
    for q in range(2):
        re, im = u[:HALF, HALF * q : HALF * (q + 1)], u[HALF:, HALF * q : HALF * (q + 1)]
        scratch[q, pl.ds(0, HALF, stride=2), :] = jnp.where(low, re, roll(im))
        scratch[q, pl.ds(1, HALF, stride=2), :] = jnp.where(low, roll(re), im)
        lh, ll = cut(scratch[q])
        out.append(
            mm(jnp.concatenate([lh, ll], 1), jnp.concatenate([txh, txh], 0)) + mm(lh, txl)
        )
    return out


def own_kernel(core_ref, own, rho_ref, support, tyh, tyl, tw, txh, txl, out, scratch):
    core = core_ref[0]
    shares = half_planes(own, 0, tyh, tyl, tw, txh[core], txl[core], scratch)
    for q, m in enumerate(shares):
        rho = rho_ref[q].astype(jnp.float32)
        mask = support[q].astype(jnp.float32)
        out[q] = rho + mask * (2.0 * m - rho) - m


def update_kernel(core_ref, partial, other, support, tyh, tyl, tw, txh, txl, out, scratch):
    core = 1 - core_ref[0]
    shares = half_planes(other, 2, tyh, tyl, tw, txh[core], txl[core], scratch)
    for q, m in enumerate(shares):
        mask = support[q].astype(jnp.float32)
        out[q] = (partial[q] + (2.0 * mask - 1.0) * m).astype(jnp.bfloat16)


SMEM = pl.BlockSpec(memory_space=pltpu.SMEM)
VMEM = pl.BlockSpec(memory_space=pltpu.VMEM)


def call(kernel, out_shape, operands, in_specs, flops, out_specs=VMEM, **more):
    return pl.pallas_call(
        kernel,
        out_shape=out_shape,
        in_specs=in_specs,
        out_specs=out_specs,
        compiler_params=pltpu.CompilerParams(vmem_limit_bytes=40 * 2**20),
        cost_estimate=pl.CostEstimate(
            flops=int(flops), bytes_accessed=2 * 2**20, transcendentals=0
        ),
        **more,
    )(*operands)


def shards(density, amplitudes, support):
    c = {k: jax.tree.map(jnp.asarray, v) for k, v in constants().items()}
    swap = [(i, i ^ 1) for i in range(2 * CHIPS)]
    same_core = [[int(2 * chip + core) for chip in ORDER] for core in range(2)]
    core = (lax.axis_index("slab") % 2).astype(jnp.int32).reshape(1)

    def exchange(x):
        return lax.all_to_all(
            x, "slab", split_axis=0, concat_axis=0, tiled=True, axis_index_groups=same_core
        )

    def shape(dims, kind):
        return jax.ShapeDtypeStruct(dims, kind)

    density_other = lax.ppermute(density, "slab", swap)
    amplitudes_other = lax.ppermute(amplitudes, "slab", swap)
    table = lax.dynamic_index_in_dim(c["first"], core[0], 0, keepdims=False)
    sent = call(
        forward_kernel,
        shape((CHIPS * 16, HALF), jnp.int32),
        (density, amplitudes, density_other, amplitudes_other, table, c["tw"]),
        [VMEM] * 6,
        800e6,
        scratch_shapes=[pltpu.VMEM((4, N, HALF), jnp.float32)],
    )
    lines = exchange(sent.reshape(CHIPS, 16, HALF)).reshape(CHIPS * 16, HALF)
    sent = call(
        middle_kernel,
        shape((CHIPS * 8, HALF), jnp.int32),
        (core, lines, *c["tz"], *c["tzi"], c["tzw"], c["rev_all"]),
        [SMEM] + [VMEM] * 7,
        800e6,
    )
    planes = exchange(sent.reshape(CHIPS, 8, HALF)).reshape(CHIPS * 8, HALF)
    planes_other = lax.ppermute(planes, "slab", swap)
    tables = (*c["tyi"], c["tw"], *c["txi"])
    partial = call(
        own_kernel,
        shape(density.shape, jnp.float32),
        (core, planes, density, support, *tables),
        [SMEM] + [VMEM] * 8,
        400e6,
        scratch_shapes=[pltpu.VMEM((2, N, HALF), jnp.float32)],
    )
    return call(
        update_kernel,
        shape(density.shape, jnp.bfloat16),
        (core, partial, planes_other, support, *tables),
        [SMEM] + [VMEM] * 8,
        400e6,
        scratch_shapes=[pltpu.VMEM((2, N, HALF), jnp.float32)],
    )


def solution(mesh):
    spec = P("slab", "member", None)
    return jax.shard_map(
        shards, mesh=mesh, in_specs=(spec, spec, spec), out_specs=spec, check_vma=False
    )
```

```python
import functools

import jax
import jax.numpy as jnp
import ml_dtypes
import numpy as np
from jax import lax
from jax.experimental import pallas as pl
from jax.experimental.pallas import tpu as pltpu
from jax.sharding import PartitionSpec as P

N = 256
CHIPS = 64
HALF = N // 2
QUARTER = N // 4
FLOOR = 0.25
FULL = 16380.0
FORWARD_LOW = -20
INVERSE_LOW = -25
AMP_UNIT = 512.0
ORDER = np.arange(CHIPS) ^ 44


def angles(k, position):
    turns = np.outer(2 * np.asarray(k) - (N - 1), np.asarray(position)) % (2 * N)
    return turns * (np.pi / N)


def split(table):
    high = table.astype(ml_dtypes.bfloat16)
    low = (table - high.astype(np.float64)).astype(ml_dtypes.bfloat16)
    return high, low


def two(tables):
    highs, lows = zip(*(split(t) for t in tables))
    return np.stack(highs), np.stack(lows)


def turned(c, s):
    return np.concatenate([np.concatenate([c, -s], 1), np.concatenate([s, c], 1)], 0)


@functools.cache
def constants():
    out = {}
    scale = 1.0 / np.sqrt(N)
    every = np.arange(N)
    half = np.arange(HALF)
    a = angles(half, 2 * half)
    ty = turned(np.cos(a), -np.sin(a)) * scale
    out["tyi"] = split(turned(np.cos(a.T), np.sin(a.T)) * scale)
    lanes = np.repeat([0, 1], QUARTER)
    a = angles(half, lanes)
    out["tw"] = np.stack([np.cos(a), np.sin(a)]).astype(np.float32)
    first, inverse = [], []
    rev = np.zeros((HALF, N))
    rev[:, :HALF] = np.eye(HALF)[::-1]
    for core in range(2):
        kx = np.arange(QUARTER) + QUARTER * core
        a = angles(kx, every)
        tx = np.concatenate([np.cos(a), -np.sin(a)], 0)
        inverse.append(tx * (2.0 * scale))
        pick = np.zeros((N, N))
        for h in range(2):
            pick[kx, QUARTER * h + np.arange(QUARTER)] = 1
            pick[N - 1 - kx, HALF + QUARTER * h + np.arange(QUARTER)] = 1
        parts = [np.concatenate(split(tx.T * scale), 1), *split(ty), pick, rev]
        first.append(np.concatenate([p.astype(ml_dtypes.bfloat16) for p in parts], 0))
    out["first"] = np.stack(first)
    out["txi"] = two(inverse)
    forward, inverse, twist = [], [], []
    for core in range(2):
        planes = [0, 1, 2, 3] if core == 0 else [2, 3, 0, 1]
        kz = np.concatenate([4 * ORDER[CHIPS // 2 :] + p for p in planes])
        z = np.concatenate([4 * ORDER + p for p in planes[::2]])
        a = angles(kz, z)
        forward.append(turned(np.cos(a), -np.sin(a)) * scale)
        inverse.append(turned(np.cos(a.T), np.sin(a.T)) * scale)
        a = angles(kz, np.ones(HALF, int))
        twist.append(np.stack([np.cos(a), np.sin(a)]))
        kz = np.concatenate([kz, kz + HALF])
        out["rev_all"] = (kz[:, None] + kz[None, :] == N - 1).astype(ml_dtypes.bfloat16)
    out["tz"] = two(forward)
    out["tzi"] = two(inverse)
    out["tzw"] = np.stack(twist).astype(np.float32)
    return out


def mm(a, b):
    return jnp.dot(a, b, preferred_element_type=jnp.float32)


def cut(x):
    high = x.astype(jnp.bfloat16)
    return high, (x - high.astype(jnp.float32)).astype(jnp.bfloat16)


def left3(high, low, x):
    xh, xl = cut(x)
    return mm(high, xh) + (mm(high, xl) + mm(low, xh))


def pack(re0, im0, re1, im1, low):
    m = jnp.maximum(jnp.maximum(jnp.abs(re0), jnp.abs(im0)), jnp.maximum(jnp.abs(re1), jnp.abs(im1)))
    e = jnp.clip(jnp.floor(jnp.log2(jnp.maximum(m, 1e-30))) + (1.0 - low), 0.0, 31.0)
    s = jnp.exp2(-(e + low)) * FULL
    e = e.astype(jnp.int32)

    def code(x, factor, middle):
        return (x * factor + (middle + 0.5)).astype(jnp.int32)

    word0 = (code(re0, s, 16384) << 17) | (code(im0, s, 16384) << 2) | (e & 3)
    word1 = (code(re1, s, 16384) << 17) | (code(im1, 0.5 * s, 8192) << 3) | (e >> 2)
    return word0, word1


def unpack(word0, word1, low):
    e = (word0 & 3) | ((word1 & 7) << 2)
    s = jnp.exp2(e.astype(jnp.float32) + low) * (1.0 / FULL)

    def value(code, factor, middle):
        return (code - middle).astype(jnp.float32) * factor

    re0 = value(lax.shift_right_logical(word0, 17), s, 16384)
    im0 = value((word0 >> 2) & 0x7FFF, s, 16384)
    re1 = value(lax.shift_right_logical(word1, 17), s, 16384)
    im1 = value((word1 >> 3) & 0x3FFF, 2.0 * s, 8192)
    return re0, im0, re1, im1


def roll(x):
    return pltpu.roll(x, QUARTER, 1)


def lower(rows):
    return lax.broadcasted_iota(jnp.int32, (rows, HALF), 1) < QUARTER


def butterfly(x, low):
    return roll(x) + jnp.where(low, x, -x)


def square(x):
    return jnp.concatenate(
        [jnp.concatenate([x[0], x[2]], 1), jnp.concatenate([x[1], x[3]], 1)], 0
    )


def forward_kernel(rho_own, amp_own, rho_other, amp_other, table, tw, out, scratch):
    low = lower(HALF)
    c, s = tw[0], tw[1]
    rho = [rho_own[0], rho_own[1], rho_other[0], rho_other[1]]
    amp = [amp_own[0], amp_own[1], amp_other[0], amp_other[1]]

    def along_x(p):
        a = mm(rho[p], table[:N])
        scratch[p] = a[:, :HALF] + a[:, HALF:]
        even = scratch[p, pl.ds(0, HALF, stride=2), :]
        odd = scratch[p, pl.ds(1, HALF, stride=2), :]
        return [jnp.where(low, even, roll(odd)), jnp.where(low, roll(even), odd)]

    def along_y(stack):
        u = left3(table[N : 2 * N], table[2 * N : 3 * N], square(stack))
        parts = []
        for q in range(2):
            re, im = u[:HALF, HALF * q : HALF * (q + 1)], u[HALF:, HALF * q : HALF * (q + 1)]
            parts += [butterfly(re * c + im * s, low), butterfly(im * c - re * s, low)]
        return parts

    def picked(p):
        both = mm(amp[p], table[3 * N : 4 * N])
        direct = jnp.where(low, both[:HALF, :HALF], both[HALF:, :HALF])
        return direct, jnp.where(low, both[HALF:, HALF:], both[:HALF, HALF:])

    def store(slot, words):
        for r in range(2):
            out[pl.ds(slot + r, CHIPS, stride=16), :] = words[CHIPS * r : CHIPS * (r + 1)]

    lines = [along_x(p) for p in range(4)]
    first = along_y(lines[0] + lines[1])
    directs, mirrors = zip(*(picked(p) for p in range(4)))
    second = along_y(lines[2] + lines[3])
    for q, words in enumerate(pack(*first, FORWARD_LOW)):
        store(2 * q, words)
    mirrors = mm(table[4 * N :, :HALF], jnp.concatenate(mirrors, 1).astype(jnp.bfloat16))
    for p in range(4):
        mirror = (mirrors[:, HALF * p : HALF * (p + 1)] * AMP_UNIT).astype(jnp.int32)
        store(8 + 2 * p, ((directs[p] * AMP_UNIT).astype(jnp.int32) << 16) | mirror)
    for q, words in enumerate(pack(*second, FORWARD_LOW)):
        store(4 + 2 * q, words)


def middle_kernel(core_ref, msg, tzh, tzl, tzih, tzil, tzw, rev, out):
    core = core_ref[0]
    c, s = tzw[core, 0], tzw[core, 1]
    half = CHIPS // 2
    spectra, mirrors, directs = [], [], []
    for r in range(2):
        parts = []
        for p in (0, 2):
            pair = [msg[pl.ds(2 * (p + i) + r, CHIPS, stride=16), :] for i in range(2)]
            parts.append(unpack(*pair, FORWARD_LOW))
        lines = square([jnp.concatenate(x, 0) for x in zip(*parts)])
        u = left3(tzh[core], tzl[core], lines)
        even_re, odd_re = u[:HALF, :HALF], u[:HALF, HALF:]
        even_im, odd_im = u[HALF:, :HALF], u[HALF:, HALF:]
        odd_re, odd_im = odd_re * c + odd_im * s, odd_im * c - odd_re * s
        spectra.append(
            (
                jnp.concatenate([even_re + odd_re, even_re - odd_re], 0),
                jnp.concatenate([even_im + odd_im, even_im - odd_im], 0),
            )
        )
        coded = jnp.concatenate(
            [
                msg[pl.ds(16 * chip + 8 + 2 * p + r, half, stride=16), :]
                for chip in (half, 0)
                for p in range(4)
            ],
            0,
        )
        directs.append((coded >> 16).astype(jnp.float32))
        mirrors.append((coded & 0xFFFF).astype(jnp.float32).astype(jnp.bfloat16))
    mirrors = mm(rev[...], jnp.concatenate(mirrors, 1))
    for r in range(2):
        re, im = spectra[r]
        target = (directs[r] + mirrors[:, HALF * r : HALF * (r + 1)]) * (0.5 / AMP_UNIT)
        ratio = target * lax.rsqrt(jnp.maximum(re * re + im * im, FLOOR * FLOOR))
        re, im = re * ratio, im * ratio
        odd_re, odd_im = re[:HALF] - re[HALF:], im[:HALF] - im[HALF:]
        lines = square(
            [
                re[:HALF] + re[HALF:],
                im[:HALF] + im[HALF:],
                odd_re * c - odd_im * s,
                odd_im * c + odd_re * s,
            ]
        )
        u = left3(tzih[core], tzil[core], lines)
        for i in range(2):
            re, im = u[CHIPS * i : CHIPS * (i + 1)], u[HALF + CHIPS * i : HALF + CHIPS * (i + 1)]
            words = pack(re[:, :HALF], im[:, :HALF], re[:, HALF:], im[:, HALF:], INVERSE_LOW)
            for o in range(2):
                out[pl.ds(2 * (2 * i + o) + r, CHIPS, stride=8), :] = words[o]


def give_kernel(planes, out):
    for slot in range(4):
        out[pl.ds(slot, CHIPS, stride=4), :] = planes[pl.ds(4 + slot, CHIPS, stride=8), :]


def half_planes(ref, stride, tyh, tyl, tw, txh, txl, scratch):
    low = lower(HALF)
    c, s = tw[0], tw[1]
    words = [
        jnp.concatenate([ref[pl.ds(2 * p + r, CHIPS, stride=stride), :] for r in range(2)], 0)
        for p in range(2)
    ]
    parts = unpack(*words, INVERSE_LOW)
    stack = []
    for q in range(2):
        re, im = (butterfly(x, low) for x in parts[2 * q : 2 * q + 2])
        stack += [re * c - im * s, im * c + re * s]
    u = left3(tyh[...], tyl[...], square(stack))
    out = []
    for q in range(2):
        re, im = u[:HALF, HALF * q : HALF * (q + 1)], u[HALF:, HALF * q : HALF * (q + 1)]
        scratch[q, pl.ds(0, HALF, stride=2), :] = jnp.where(low, re, roll(im))
        scratch[q, pl.ds(1, HALF, stride=2), :] = jnp.where(low, roll(re), im)
        lh, ll = cut(scratch[q])
        out.append(
            mm(jnp.concatenate([lh, ll], 1), jnp.concatenate([txh, txh], 0)) + mm(lh, txl)
        )
    return out


def own_kernel(core_ref, own, rho_ref, support, tyh, tyl, tw, txh, txl, out, scratch):
    core = core_ref[0]
    shares = half_planes(own, 8, tyh, tyl, tw, txh[core], txl[core], scratch)
    for q, m in enumerate(shares):
        rho = rho_ref[q].astype(jnp.float32)
        mask = support[q].astype(jnp.float32)
        out[q] = rho + mask * (2.0 * m - rho) - m


def update_kernel(core_ref, partial, other, support, tyh, tyl, tw, txh, txl, out, scratch):
    core = 1 - core_ref[0]
    shares = half_planes(other, 4, tyh, tyl, tw, txh[core], txl[core], scratch)
    for q, m in enumerate(shares):
        mask = support[q].astype(jnp.float32)
        out[q] = (partial[q] + (2.0 * mask - 1.0) * m).astype(jnp.bfloat16)


SMEM = pl.BlockSpec(memory_space=pltpu.SMEM)
VMEM = pl.BlockSpec(memory_space=pltpu.VMEM)


def call(kernel, out_shape, operands, in_specs, flops, out_specs=VMEM, **more):
    return pl.pallas_call(
        kernel,
        out_shape=out_shape,
        in_specs=in_specs,
        out_specs=out_specs,
        compiler_params=pltpu.CompilerParams(vmem_limit_bytes=40 * 2**20),
        cost_estimate=pl.CostEstimate(
            flops=int(flops), bytes_accessed=2 * 2**20, transcendentals=0
        ),
        **more,
    )(*operands)


def shards(density, amplitudes, support):
    c = {k: jax.tree.map(jnp.asarray, v) for k, v in constants().items()}
    swap = [(i, i ^ 1) for i in range(2 * CHIPS)]
    same_core = [[int(2 * chip + core) for chip in ORDER] for core in range(2)]
    core = (lax.axis_index("slab") % 2).astype(jnp.int32).reshape(1)

    def exchange(x):
        return lax.all_to_all(
            x, "slab", split_axis=0, concat_axis=0, tiled=True, axis_index_groups=same_core
        )

    def shape(dims, kind):
        return jax.ShapeDtypeStruct(dims, kind)

    density_other = lax.ppermute(density, "slab", swap)
    amplitudes_other = lax.ppermute(amplitudes, "slab", swap)
    table = lax.dynamic_index_in_dim(c["first"], core[0], 0, keepdims=False)
    sent = call(
        forward_kernel,
        shape((CHIPS * 16, HALF), jnp.int32),
        (density, amplitudes, density_other, amplitudes_other, table, c["tw"]),
        [VMEM] * 6,
        800e6,
        scratch_shapes=[pltpu.VMEM((4, N, HALF), jnp.float32)],
    )
    lines = exchange(sent.reshape(CHIPS, 16, HALF)).reshape(CHIPS * 16, HALF)
    sent = call(
        middle_kernel,
        shape((CHIPS * 8, HALF), jnp.int32),
        (core, lines, *c["tz"], *c["tzi"], c["tzw"], c["rev_all"]),
        [SMEM] + [VMEM] * 7,
        800e6,
    )
    planes = exchange(sent.reshape(CHIPS, 8, HALF)).reshape(CHIPS * 8, HALF)
    given = call(give_kernel, shape((CHIPS * 4, HALF), jnp.int32), (planes,), [VMEM], 1e5)
    planes_other = lax.ppermute(given, "slab", swap)
    tables = (*c["tyi"], c["tw"], *c["txi"])
    partial = call(
        own_kernel,
        shape(density.shape, jnp.float32),
        (core, planes, density, support, *tables),
        [SMEM] + [VMEM] * 8,
        400e6,
        scratch_shapes=[pltpu.VMEM((2, N, HALF), jnp.float32)],
    )
    return call(
        update_kernel,
        shape(density.shape, jnp.bfloat16),
        (core, partial, planes_other, support, *tables),
        [SMEM] + [VMEM] * 8,
        400e6,
        scratch_shapes=[pltpu.VMEM((2, N, HALF), jnp.float32)],
    )


def solution(mesh):
    spec = P("slab", "member", None)
    return jax.shard_map(
        shards, mesh=mesh, in_specs=(spec, spec, spec), out_specs=spec, check_vma=False
    )
```

```python
import functools

import jax
import jax.numpy as jnp
import ml_dtypes
import numpy as np
from jax import lax
from jax.experimental import pallas as pl
from jax.experimental.pallas import tpu as pltpu
from jax.sharding import PartitionSpec as P

N = 256
CHIPS = 64
HALF = N // 2
QUARTER = N // 4
FLOOR = 0.25
FULL = 16380.0
FORWARD_LOW = -20
INVERSE_LOW = -25
AMP_UNIT = 512.0
ORDER = np.arange(CHIPS) ^ 44


def angles(k, position):
    turns = np.outer(2 * np.asarray(k) - (N - 1), np.asarray(position)) % (2 * N)
    return turns * (np.pi / N)


def split(table):
    high = table.astype(ml_dtypes.bfloat16)
    low = (table - high.astype(np.float64)).astype(ml_dtypes.bfloat16)
    return high, low


def two(tables):
    highs, lows = zip(*(split(t) for t in tables))
    return np.stack(highs), np.stack(lows)


def turned(c, s):
    return np.concatenate([np.concatenate([c, -s], 1), np.concatenate([s, c], 1)], 0)


@functools.cache
def constants():
    out = {}
    scale = 1.0 / np.sqrt(N)
    every = np.arange(N)
    half = np.arange(HALF)
    a = angles(half, 2 * half)
    ty = turned(np.cos(a), -np.sin(a)) * scale
    out["tyi"] = split(turned(np.cos(a.T), np.sin(a.T)) * scale)
    lanes = np.repeat([0, 1], QUARTER)
    a = angles(half, lanes)
    out["tw"] = np.stack([np.cos(a), np.sin(a)]).astype(np.float32)
    first, inverse = [], []
    rev = np.zeros((HALF, N))
    rev[:, :HALF] = np.eye(HALF)[::-1]
    for core in range(2):
        kx = np.arange(QUARTER) + QUARTER * core
        a = angles(kx, every)
        tx = np.concatenate([np.cos(a), -np.sin(a)], 0)
        inverse.append(tx * (2.0 * scale))
        pick = np.zeros((N, N))
        for h in range(2):
            pick[kx, QUARTER * h + np.arange(QUARTER)] = 1
            pick[N - 1 - kx, HALF + QUARTER * h + np.arange(QUARTER)] = 1
        parts = [np.concatenate(split(tx.T * scale), 1), *split(ty), pick, rev]
        first.append(np.concatenate([p.astype(ml_dtypes.bfloat16) for p in parts], 0))
    out["first"] = np.stack(first)
    out["txi"] = two(inverse)
    forward, inverse, twist = [], [], []
    for core in range(2):
        planes = [0, 1, 2, 3] if core == 0 else [2, 3, 0, 1]
        kz = np.concatenate([4 * ORDER[CHIPS // 2 :] + p for p in planes])
        z = np.concatenate([4 * ORDER + p for p in planes[::2]])
        a = angles(kz, z)
        forward.append(turned(np.cos(a), -np.sin(a)) * scale)
        inverse.append(turned(np.cos(a.T), np.sin(a.T)) * scale)
        a = angles(kz, np.ones(HALF, int))
        twist.append(np.stack([np.cos(a), np.sin(a)]))
        kz = np.concatenate([kz, kz + HALF])
        out["rev_all"] = (kz[:, None] + kz[None, :] == N - 1).astype(ml_dtypes.bfloat16)
    out["tz"] = two(forward)
    out["tzi"] = two(inverse)
    out["tzw"] = np.stack(twist).astype(np.float32)
    return out


def mm(a, b):
    return jnp.dot(a, b, preferred_element_type=jnp.float32)


def cut(x):
    high = x.astype(jnp.bfloat16)
    return high, (x - high.astype(jnp.float32)).astype(jnp.bfloat16)


def left3(high, low, x):
    xh, xl = cut(x)
    return mm(high, xh) + (mm(high, xl) + mm(low, xh))


def pack(re0, im0, re1, im1, low):
    m = jnp.maximum(jnp.maximum(jnp.abs(re0), jnp.abs(im0)), jnp.maximum(jnp.abs(re1), jnp.abs(im1)))
    e = jnp.clip(jnp.floor(jnp.log2(jnp.maximum(m, 1e-30))) + (1.0 - low), 0.0, 31.0)
    s = jnp.exp2(-(e + low)) * FULL
    e = e.astype(jnp.int32)

    def code(x, factor, middle):
        return (x * factor + (middle + 0.5)).astype(jnp.int32)

    word0 = (code(re0, s, 16384) << 17) | (code(im0, s, 16384) << 2) | (e & 3)
    word1 = (code(re1, s, 16384) << 17) | (code(im1, 0.5 * s, 8192) << 3) | (e >> 2)
    return word0, word1


def unpack(word0, word1, low):
    e = (word0 & 3) | ((word1 & 7) << 2)
    s = jnp.exp2(e.astype(jnp.float32) + low) * (1.0 / FULL)

    def value(code, factor, middle):
        return (code - middle).astype(jnp.float32) * factor

    re0 = value(lax.shift_right_logical(word0, 17), s, 16384)
    im0 = value((word0 >> 2) & 0x7FFF, s, 16384)
    re1 = value(lax.shift_right_logical(word1, 17), s, 16384)
    im1 = value((word1 >> 3) & 0x3FFF, 2.0 * s, 8192)
    return re0, im0, re1, im1


def roll(x):
    return pltpu.roll(x, QUARTER, 1)


def lower(rows):
    return lax.broadcasted_iota(jnp.int32, (rows, HALF), 1) < QUARTER


def butterfly(x, low):
    return roll(x) + jnp.where(low, x, -x)


def square(x):
    return jnp.concatenate(
        [jnp.concatenate([x[0], x[2]], 1), jnp.concatenate([x[1], x[3]], 1)], 0
    )


def forward_kernel(rho_own, amp_own, rho_other, amp_other, table, tw, out, scratch):
    low = lower(HALF)
    c, s = tw[0], tw[1]
    rho = [rho_own[0], rho_own[1], rho_other[0], rho_other[1]]
    amp = [amp_own[0], amp_own[1], amp_other[0], amp_other[1]]

    def along_x(p):
        a = mm(rho[p], table[:N])
        scratch[p] = a[:, :HALF] + a[:, HALF:]
        even = scratch[p, pl.ds(0, HALF, stride=2), :]
        odd = scratch[p, pl.ds(1, HALF, stride=2), :]
        return [jnp.where(low, even, roll(odd)), jnp.where(low, roll(even), odd)]

    def along_y(stack):
        u = left3(table[N : 2 * N], table[2 * N : 3 * N], square(stack))
        parts = []
        for q in range(2):
            re, im = u[:HALF, HALF * q : HALF * (q + 1)], u[HALF:, HALF * q : HALF * (q + 1)]
            parts += [butterfly(re * c + im * s, low), butterfly(im * c - re * s, low)]
        return parts

    def picked(p):
        both = mm(amp[p], table[3 * N : 4 * N])
        direct = jnp.where(low, both[:HALF, :HALF], both[HALF:, :HALF])
        return direct, jnp.where(low, both[HALF:, HALF:], both[:HALF, HALF:])

    def store(slot, words):
        for r in range(2):
            out[pl.ds(slot + r, CHIPS, stride=16), :] = words[CHIPS * r : CHIPS * (r + 1)]

    lines = [along_x(p) for p in range(4)]
    first = along_y(lines[0] + lines[1])
    directs, mirrors = zip(*(picked(p) for p in range(4)))
    second = along_y(lines[2] + lines[3])
    for q, words in enumerate(pack(*first, FORWARD_LOW)):
        store(2 * q, words)
    mirrors = mm(table[4 * N :, :HALF], jnp.concatenate(mirrors, 1).astype(jnp.bfloat16))
    for p in range(4):
        mirror = (mirrors[:, HALF * p : HALF * (p + 1)] * AMP_UNIT).astype(jnp.int32)
        store(8 + 2 * p, ((directs[p] * AMP_UNIT).astype(jnp.int32) << 16) | mirror)
    for q, words in enumerate(pack(*second, FORWARD_LOW)):
        store(4 + 2 * q, words)


def middle_kernel(core_ref, msg, tzh, tzl, tzih, tzil, tzw, rev, out):
    core = core_ref[0]
    c, s = tzw[core, 0], tzw[core, 1]
    half = CHIPS // 2
    spectra, mirrors, directs = [], [], []
    for r in range(2):
        parts = []
        for p in (0, 2):
            pair = [msg[pl.ds(2 * (p + i) + r, CHIPS, stride=16), :] for i in range(2)]
            parts.append(unpack(*pair, FORWARD_LOW))
        lines = square([jnp.concatenate(x, 0) for x in zip(*parts)])
        u = left3(tzh[core], tzl[core], lines)
        even_re, odd_re = u[:HALF, :HALF], u[:HALF, HALF:]
        even_im, odd_im = u[HALF:, :HALF], u[HALF:, HALF:]
        odd_re, odd_im = odd_re * c + odd_im * s, odd_im * c - odd_re * s
        spectra.append(
            (
                jnp.concatenate([even_re + odd_re, even_re - odd_re], 0),
                jnp.concatenate([even_im + odd_im, even_im - odd_im], 0),
            )
        )
        coded = jnp.concatenate(
            [
                msg[pl.ds(16 * chip + 8 + 2 * p + r, half, stride=16), :]
                for chip in (half, 0)
                for p in range(4)
            ],
            0,
        )
        directs.append((coded >> 16).astype(jnp.float32))
        mirrors.append((coded & 0xFFFF).astype(jnp.float32).astype(jnp.bfloat16))
    mirrors = mm(rev[...], jnp.concatenate(mirrors, 1))
    for r in range(2):
        re, im = spectra[r]
        target = (directs[r] + mirrors[:, HALF * r : HALF * (r + 1)]) * (0.5 / AMP_UNIT)
        ratio = target * lax.rsqrt(jnp.maximum(re * re + im * im, FLOOR * FLOOR))
        re, im = re * ratio, im * ratio
        odd_re, odd_im = re[:HALF] - re[HALF:], im[:HALF] - im[HALF:]
        lines = square(
            [
                re[:HALF] + re[HALF:],
                im[:HALF] + im[HALF:],
                odd_re * c - odd_im * s,
                odd_im * c + odd_re * s,
            ]
        )
        u = left3(tzih[core], tzil[core], lines)
        for i in range(2):
            re, im = u[CHIPS * i : CHIPS * (i + 1)], u[HALF + CHIPS * i : HALF + CHIPS * (i + 1)]
            words = pack(re[:, :HALF], im[:, :HALF], re[:, HALF:], im[:, HALF:], INVERSE_LOW)
            for o in range(2):
                out[pl.ds(2 * (2 * i + o) + r, CHIPS, stride=8), :] = words[o]


def half_planes(ref, first, tyh, tyl, tw, txh, txl):
    low = lower(HALF)
    c, s = tw[0], tw[1]
    words = [
        jnp.concatenate([ref[pl.ds(2 * p + r, CHIPS, stride=8), :] for r in range(2)], 0)
        for p in (first, first + 1)
    ]
    parts = unpack(*words, INVERSE_LOW)
    stack = []
    for q in range(2):
        re, im = (butterfly(x, low) for x in parts[2 * q : 2 * q + 2])
        stack += [re * c - im * s, im * c + re * s]
    u = left3(tyh[...], tyl[...], square(stack))
    out = []
    for q in range(2):
        re, im = u[:HALF, HALF * q : HALF * (q + 1)], u[HALF:, HALF * q : HALF * (q + 1)]
        lines = jnp.concatenate(
            [jnp.where(low, re, roll(im)), jnp.where(low, roll(re), im)], 0
        )
        lh, ll = cut(lines)
        out.append(
            mm(jnp.concatenate([lh, ll, lh], 1), jnp.concatenate([txh, txh, txl], 0))
        )
    return out


def interleave(rows, side, scratch):
    for o in range(2):
        scratch[pl.ds(o, HALF, stride=2), :] = rows[
            HALF * o : HALF * (o + 1), HALF * side : HALF * (side + 1)
        ]
    return scratch[...]


def own_kernel(core_ref, own, rho_ref, support, tyh, tyl, tw, txh, txl, out, scratch):
    core = core_ref[0]
    for q, term in enumerate(half_planes(own, 0, tyh, tyl, tw, txh[core], txl[core])):
        for side in range(2):
            lanes = slice(HALF * side, HALF * (side + 1))
            m = interleave(term, side, scratch.at[2 * q + side])
            rho = rho_ref[q, :, lanes].astype(jnp.float32)
            mask = support[q, :, lanes].astype(jnp.float32)
            out[q, :, lanes] = rho + mask * (2.0 * m - rho) - m


def update_kernel(core_ref, partial, other, support, tyh, tyl, tw, txh, txl, out, scratch, done, sems):
    core = 1 - core_ref[0]
    copies = []
    for q, term in enumerate(half_planes(other, 2, tyh, tyl, tw, txh[core], txl[core])):
        for side in range(2):
            lanes = slice(HALF * side, HALF * (side + 1))
            m = interleave(term, side, scratch.at[2 * q + side])
            mask = support[q, :, lanes].astype(jnp.float32)
            done[q, :, lanes] = (partial[q, :, lanes] + (2.0 * mask - 1.0) * m).astype(jnp.bfloat16)
        copies.append(pltpu.make_async_copy(done.at[q], out.at[q], sems.at[q]))
        copies[q].start()
    for copy in copies:
        copy.wait()


SMEM = pl.BlockSpec(memory_space=pltpu.SMEM)
VMEM = pl.BlockSpec(memory_space=pltpu.VMEM)
HBM = pl.BlockSpec(memory_space=pltpu.HBM)


def call(kernel, out_shape, operands, in_specs, flops, out_specs=VMEM, **more):
    return pl.pallas_call(
        kernel,
        out_shape=out_shape,
        in_specs=in_specs,
        out_specs=out_specs,
        compiler_params=pltpu.CompilerParams(vmem_limit_bytes=40 * 2**20),
        cost_estimate=pl.CostEstimate(
            flops=int(flops), bytes_accessed=2 * 2**20, transcendentals=0
        ),
        **more,
    )(*operands)


def shards(density, amplitudes, support):
    c = {k: jax.tree.map(jnp.asarray, v) for k, v in constants().items()}
    swap = [(i, i ^ 1) for i in range(2 * CHIPS)]
    same_core = [[int(2 * chip + core) for chip in ORDER] for core in range(2)]
    core = (lax.axis_index("slab") % 2).astype(jnp.int32).reshape(1)

    def exchange(x):
        return lax.all_to_all(
            x, "slab", split_axis=0, concat_axis=0, tiled=True, axis_index_groups=same_core
        )

    def shape(dims, kind):
        return jax.ShapeDtypeStruct(dims, kind)

    density_other = lax.ppermute(density, "slab", swap)
    amplitudes_other = lax.ppermute(amplitudes, "slab", swap)
    table = lax.dynamic_index_in_dim(c["first"], core[0], 0, keepdims=False)
    sent = call(
        forward_kernel,
        shape((CHIPS * 16, HALF), jnp.int32),
        (density, amplitudes, density_other, amplitudes_other, table, c["tw"]),
        [VMEM] * 6,
        800e6,
        scratch_shapes=[pltpu.VMEM((4, N, HALF), jnp.float32)],
    )
    lines = exchange(sent.reshape(CHIPS, 16, HALF)).reshape(CHIPS * 16, HALF)
    sent = call(
        middle_kernel,
        shape((CHIPS * 8, HALF), jnp.int32),
        (core, lines, *c["tz"], *c["tzi"], c["tzw"], c["rev_all"]),
        [SMEM] + [VMEM] * 7,
        800e6,
    )
    planes = exchange(sent.reshape(CHIPS, 8, HALF)).reshape(CHIPS * 8, HALF)
    planes_other = lax.ppermute(planes, "slab", swap)
    tables = (*c["tyi"], c["tw"], *c["txi"])
    partial = call(
        own_kernel,
        shape(density.shape, jnp.float32),
        (core, planes, density, support, *tables),
        [SMEM] + [VMEM] * 8,
        400e6,
        scratch_shapes=[pltpu.VMEM((4, N, HALF), jnp.float32)],
    )
    return call(
        update_kernel,
        shape(density.shape, jnp.bfloat16),
        (core, partial, planes_other, support, *tables),
        [SMEM] + [VMEM] * 8,
        400e6,
        out_specs=HBM,
        scratch_shapes=[
            pltpu.VMEM((4, N, HALF), jnp.float32),
            pltpu.VMEM(density.shape, jnp.bfloat16),
            pltpu.SemaphoreType.DMA((2,)),
        ],
    )


def solution(mesh):
    spec = P("slab", "member", None)
    return jax.shard_map(
        shards, mesh=mesh, in_specs=(spec, spec, spec), out_specs=spec, check_vma=False
    )
```

```python
import functools

import jax
import jax.numpy as jnp
import ml_dtypes
import numpy as np
from jax import lax
from jax.experimental import pallas as pl
from jax.experimental.pallas import tpu as pltpu
from jax.sharding import PartitionSpec as P

N = 256
CHIPS = 64
HALF = N // 2
QUARTER = N // 4
FLOOR = 0.25
FULL = 16380.0
FORWARD_LOW = -20
INVERSE_LOW = -25
AMP_UNIT = 512.0
ORDER = np.arange(CHIPS) ^ 44


def angles(k, position):
    turns = np.outer(2 * np.asarray(k) - (N - 1), np.asarray(position)) % (2 * N)
    return turns * (np.pi / N)


def split(table):
    high = table.astype(ml_dtypes.bfloat16)
    low = (table - high.astype(np.float64)).astype(ml_dtypes.bfloat16)
    return high, low


def two(tables):
    highs, lows = zip(*(split(t) for t in tables))
    return np.stack(highs), np.stack(lows)


def turned(c, s):
    return np.concatenate([np.concatenate([c, -s], 1), np.concatenate([s, c], 1)], 0)


@functools.cache
def constants():
    out = {}
    scale = 1.0 / np.sqrt(N)
    every = np.arange(N)
    half = np.arange(HALF)
    a = angles(half, 2 * half)
    ty = turned(np.cos(a), -np.sin(a)) * scale
    out["tyi"] = split(turned(np.cos(a.T), np.sin(a.T)) * scale)
    lanes = np.repeat([0, 1], QUARTER)
    a = angles(half, lanes)
    out["tw"] = np.stack([np.cos(a), np.sin(a)]).astype(np.float32)
    first, inverse = [], []
    rev = np.zeros((HALF, N))
    rev[:, :HALF] = np.eye(HALF)[::-1]
    for core in range(2):
        kx = np.arange(QUARTER) + QUARTER * core
        a = angles(kx, every)
        tx = np.concatenate([np.cos(a), -np.sin(a)], 0)
        inverse.append(tx * (2.0 * scale))
        pick = np.zeros((N, N))
        for h in range(2):
            pick[kx, QUARTER * h + np.arange(QUARTER)] = 1
            pick[N - 1 - kx, HALF + QUARTER * h + np.arange(QUARTER)] = 1
        parts = [np.concatenate(split(tx.T * scale), 1), *split(ty), pick, rev]
        first.append(np.concatenate([p.astype(ml_dtypes.bfloat16) for p in parts], 0))
    out["first"] = np.stack(first)
    out["txi"] = two(inverse)
    forward, inverse, twist = [], [], []
    for core in range(2):
        planes = [0, 1, 2, 3] if core == 0 else [2, 3, 0, 1]
        kz = np.concatenate([4 * ORDER[CHIPS // 2 :] + p for p in planes])
        z = np.concatenate([4 * ORDER + p for p in planes[::2]])
        a = angles(kz, z)
        forward.append(turned(np.cos(a), -np.sin(a)) * scale)
        inverse.append(turned(np.cos(a.T), np.sin(a.T)) * scale)
        a = angles(kz, np.ones(HALF, int))
        twist.append(np.stack([np.cos(a), np.sin(a)]))
        kz = np.concatenate([kz, kz + HALF])
        out["rev_all"] = (kz[:, None] + kz[None, :] == N - 1).astype(ml_dtypes.bfloat16)
    out["tz"] = two(forward)
    out["tzi"] = two(inverse)
    out["tzw"] = np.stack(twist).astype(np.float32)
    return out


def mm(a, b):
    return jnp.dot(a, b, preferred_element_type=jnp.float32)


def cut(x):
    high = x.astype(jnp.bfloat16)
    return high, (x - high.astype(jnp.float32)).astype(jnp.bfloat16)


def left3(high, low, x):
    xh, xl = cut(x)
    return mm(high, xh) + (mm(high, xl) + mm(low, xh))


def pack(re0, im0, re1, im1, low):
    m = jnp.maximum(jnp.maximum(jnp.abs(re0), jnp.abs(im0)), jnp.maximum(jnp.abs(re1), jnp.abs(im1)))
    e = jnp.clip(jnp.floor(jnp.log2(jnp.maximum(m, 1e-30))) + (1.0 - low), 0.0, 31.0)
    s = jnp.exp2(-(e + low)) * FULL
    e = e.astype(jnp.int32)

    def code(x, factor, middle):
        return (x * factor + (middle + 0.5)).astype(jnp.int32)

    word0 = (code(re0, s, 16384) << 17) | (code(im0, s, 16384) << 2) | (e & 3)
    word1 = (code(re1, s, 16384) << 17) | (code(im1, 0.5 * s, 8192) << 3) | (e >> 2)
    return word0, word1


def unpack(word0, word1, low):
    e = (word0 & 3) | ((word1 & 7) << 2)
    s = jnp.exp2(e.astype(jnp.float32) + low) * (1.0 / FULL)

    def value(code, factor, middle):
        return (code - middle).astype(jnp.float32) * factor

    re0 = value(lax.shift_right_logical(word0, 17), s, 16384)
    im0 = value((word0 >> 2) & 0x7FFF, s, 16384)
    re1 = value(lax.shift_right_logical(word1, 17), s, 16384)
    im1 = value((word1 >> 3) & 0x3FFF, 2.0 * s, 8192)
    return re0, im0, re1, im1


def roll(x):
    return pltpu.roll(x, QUARTER, 1)


def lower(rows):
    return lax.broadcasted_iota(jnp.int32, (rows, HALF), 1) < QUARTER


def butterfly(x, low):
    return roll(x) + jnp.where(low, x, -x)


def square(x):
    return jnp.concatenate(
        [jnp.concatenate([x[0], x[2]], 1), jnp.concatenate([x[1], x[3]], 1)], 0
    )


def forward_kernel(rho_own, amp_own, rho_other, amp_other, table, tw, out, scratch):
    low = lower(HALF)
    c, s = tw[0], tw[1]
    rho = [rho_own[0], rho_own[1], rho_other[0], rho_other[1]]
    amp = [amp_own[0], amp_own[1], amp_other[0], amp_other[1]]

    def along_x(p):
        a = mm(rho[p], table[:N])
        scratch[p] = a[:, :HALF] + a[:, HALF:]
        even = scratch[p, pl.ds(0, HALF, stride=2), :]
        odd = scratch[p, pl.ds(1, HALF, stride=2), :]
        return [jnp.where(low, even, roll(odd)), jnp.where(low, roll(even), odd)]

    def along_y(stack):
        u = left3(table[N : 2 * N], table[2 * N : 3 * N], square(stack))
        parts = []
        for q in range(2):
            re, im = u[:HALF, HALF * q : HALF * (q + 1)], u[HALF:, HALF * q : HALF * (q + 1)]
            parts += [butterfly(re * c + im * s, low), butterfly(im * c - re * s, low)]
        return parts

    def picked(p):
        both = mm(amp[p], table[3 * N : 4 * N])
        direct = jnp.where(low, both[:HALF, :HALF], both[HALF:, :HALF])
        return direct, jnp.where(low, both[HALF:, HALF:], both[:HALF, HALF:])

    def store(slot, words):
        for r in range(2):
            out[pl.ds(slot + r, CHIPS, stride=16), :] = words[CHIPS * r : CHIPS * (r + 1)]

    first = along_y(along_x(0) + along_x(1))
    lines = along_x(2) + along_x(3)
    directs, mirrors = zip(*(picked(p) for p in range(4)))
    second = along_y(lines)
    for q, words in enumerate(pack(*first, FORWARD_LOW)):
        store(2 * q, words)
    mirrors = mm(table[4 * N :, :HALF], jnp.concatenate(mirrors, 1).astype(jnp.bfloat16))
    for p in range(4):
        mirror = (mirrors[:, HALF * p : HALF * (p + 1)] * AMP_UNIT).astype(jnp.int32)
        store(8 + 2 * p, ((directs[p] * AMP_UNIT).astype(jnp.int32) << 16) | mirror)
    for q, words in enumerate(pack(*second, FORWARD_LOW)):
        store(4 + 2 * q, words)


def middle_kernel(core_ref, msg, tzh, tzl, tzih, tzil, tzw, rev, out):
    core = core_ref[0]
    c, s = tzw[core, 0], tzw[core, 1]
    half = CHIPS // 2
    spectra, mirrors, directs = [], [], []
    for r in range(2):
        parts = []
        for p in (0, 2):
            pair = [msg[pl.ds(2 * (p + i) + r, CHIPS, stride=16), :] for i in range(2)]
            parts.append(unpack(*pair, FORWARD_LOW))
        lines = square([jnp.concatenate(x, 0) for x in zip(*parts)])
        u = left3(tzh[core], tzl[core], lines)
        even_re, odd_re = u[:HALF, :HALF], u[:HALF, HALF:]
        even_im, odd_im = u[HALF:, :HALF], u[HALF:, HALF:]
        odd_re, odd_im = odd_re * c + odd_im * s, odd_im * c - odd_re * s
        spectra.append(
            (
                jnp.concatenate([even_re + odd_re, even_re - odd_re], 0),
                jnp.concatenate([even_im + odd_im, even_im - odd_im], 0),
            )
        )
        coded = jnp.concatenate(
            [
                msg[pl.ds(16 * chip + 8 + 2 * p + r, half, stride=16), :]
                for chip in (half, 0)
                for p in range(4)
            ],
            0,
        )
        directs.append((coded >> 16).astype(jnp.float32))
        mirrors.append((coded & 0xFFFF).astype(jnp.float32).astype(jnp.bfloat16))
    mirrors = mm(rev[...], jnp.concatenate(mirrors, 1))
    for r in range(2):
        re, im = spectra[r]
        target = (directs[r] + mirrors[:, HALF * r : HALF * (r + 1)]) * (0.5 / AMP_UNIT)
        ratio = target * lax.rsqrt(jnp.maximum(re * re + im * im, FLOOR * FLOOR))
        re, im = re * ratio, im * ratio
        odd_re, odd_im = re[:HALF] - re[HALF:], im[:HALF] - im[HALF:]
        lines = square(
            [
                re[:HALF] + re[HALF:],
                im[:HALF] + im[HALF:],
                odd_re * c - odd_im * s,
                odd_im * c + odd_re * s,
            ]
        )
        u = left3(tzih[core], tzil[core], lines)
        for i in range(2):
            re, im = u[CHIPS * i : CHIPS * (i + 1)], u[HALF + CHIPS * i : HALF + CHIPS * (i + 1)]
            words = pack(re[:, :HALF], im[:, :HALF], re[:, HALF:], im[:, HALF:], INVERSE_LOW)
            for o in range(2):
                out[pl.ds(2 * (2 * i + o) + r, CHIPS, stride=8), :] = words[o]


def half_planes(ref, first, tyh, tyl, tw, txh, txl):
    low = lower(HALF)
    c, s = tw[0], tw[1]
    words = [
        jnp.concatenate([ref[pl.ds(2 * p + r, CHIPS, stride=8), :] for r in range(2)], 0)
        for p in (first, first + 1)
    ]
    parts = unpack(*words, INVERSE_LOW)
    stack = []
    for q in range(2):
        re, im = (butterfly(x, low) for x in parts[2 * q : 2 * q + 2])
        stack += [re * c - im * s, im * c + re * s]
    u = left3(tyh[...], tyl[...], square(stack))
    out = []
    for q in range(2):
        re, im = u[:HALF, HALF * q : HALF * (q + 1)], u[HALF:, HALF * q : HALF * (q + 1)]
        lines = jnp.concatenate(
            [jnp.where(low, re, roll(im)), jnp.where(low, roll(re), im)], 0
        )
        lh, ll = cut(lines)
        out.append(
            mm(jnp.concatenate([lh, ll, lh], 1), jnp.concatenate([txh, txh, txl], 0))
        )
    return out


def interleave(rows, side, scratch):
    for o in range(2):
        scratch[pl.ds(o, HALF, stride=2), :] = rows[
            HALF * o : HALF * (o + 1), HALF * side : HALF * (side + 1)
        ]
    return scratch[...]


def own_kernel(core_ref, own, rho_ref, support, tyh, tyl, tw, txh, txl, out, scratch):
    core = core_ref[0]
    for q, term in enumerate(half_planes(own, 0, tyh, tyl, tw, txh[core], txl[core])):
        for side in range(2):
            lanes = slice(HALF * side, HALF * (side + 1))
            m = interleave(term, side, scratch.at[2 * q + side])
            rho = rho_ref[q, :, lanes].astype(jnp.float32)
            mask = support[q, :, lanes].astype(jnp.float32)
            out[q, :, lanes] = rho + mask * (2.0 * m - rho) - m


def update_kernel(core_ref, partial, other, support, tyh, tyl, tw, txh, txl, out, scratch, done, sems):
    core = 1 - core_ref[0]
    copies = []
    for q, term in enumerate(half_planes(other, 2, tyh, tyl, tw, txh[core], txl[core])):
        for side in range(2):
            lanes = slice(HALF * side, HALF * (side + 1))
            m = interleave(term, side, scratch.at[2 * q + side])
            mask = support[q, :, lanes].astype(jnp.float32)
            done[q, :, lanes] = (partial[q, :, lanes] + (2.0 * mask - 1.0) * m).astype(jnp.bfloat16)
        copies.append(pltpu.make_async_copy(done.at[q], out.at[q], sems.at[q]))
        copies[q].start()
    for copy in copies:
        copy.wait()


SMEM = pl.BlockSpec(memory_space=pltpu.SMEM)
VMEM = pl.BlockSpec(memory_space=pltpu.VMEM)
HBM = pl.BlockSpec(memory_space=pltpu.HBM)


def call(kernel, out_shape, operands, in_specs, flops, out_specs=VMEM, **more):
    return pl.pallas_call(
        kernel,
        out_shape=out_shape,
        in_specs=in_specs,
        out_specs=out_specs,
        compiler_params=pltpu.CompilerParams(vmem_limit_bytes=40 * 2**20),
        cost_estimate=pl.CostEstimate(
            flops=int(flops), bytes_accessed=2 * 2**20, transcendentals=0
        ),
        **more,
    )(*operands)


def shards(density, amplitudes, support):
    c = {k: jax.tree.map(jnp.asarray, v) for k, v in constants().items()}
    swap = [(i, i ^ 1) for i in range(2 * CHIPS)]
    same_core = [[int(2 * chip + core) for chip in ORDER] for core in range(2)]
    core = (lax.axis_index("slab") % 2).astype(jnp.int32).reshape(1)

    def exchange(x):
        return lax.all_to_all(
            x, "slab", split_axis=0, concat_axis=0, tiled=True, axis_index_groups=same_core
        )

    def shape(dims, kind):
        return jax.ShapeDtypeStruct(dims, kind)

    density_other = lax.ppermute(density, "slab", swap)
    amplitudes_other = lax.ppermute(amplitudes, "slab", swap)
    table = lax.dynamic_index_in_dim(c["first"], core[0], 0, keepdims=False)
    sent = call(
        forward_kernel,
        shape((CHIPS * 16, HALF), jnp.int32),
        (density, amplitudes, density_other, amplitudes_other, table, c["tw"]),
        [VMEM] * 6,
        800e6,
        scratch_shapes=[pltpu.VMEM((4, N, HALF), jnp.float32)],
    )
    lines = exchange(sent.reshape(CHIPS, 16, HALF)).reshape(CHIPS * 16, HALF)
    sent = call(
        middle_kernel,
        shape((CHIPS * 8, HALF), jnp.int32),
        (core, lines, *c["tz"], *c["tzi"], c["tzw"], c["rev_all"]),
        [SMEM] + [VMEM] * 7,
        800e6,
    )
    planes = exchange(sent.reshape(CHIPS, 8, HALF)).reshape(CHIPS * 8, HALF)
    planes_other = lax.ppermute(planes, "slab", swap)
    tables = (*c["tyi"], c["tw"], *c["txi"])
    partial = call(
        own_kernel,
        shape(density.shape, jnp.float32),
        (core, planes, density, support, *tables),
        [SMEM] + [VMEM] * 8,
        400e6,
        scratch_shapes=[pltpu.VMEM((4, N, HALF), jnp.float32)],
    )
    return call(
        update_kernel,
        shape(density.shape, jnp.bfloat16),
        (core, partial, planes_other, support, *tables),
        [SMEM] + [VMEM] * 8,
        400e6,
        out_specs=HBM,
        scratch_shapes=[
            pltpu.VMEM((4, N, HALF), jnp.float32),
            pltpu.VMEM(density.shape, jnp.bfloat16),
            pltpu.SemaphoreType.DMA((2,)),
        ],
    )


def solution(mesh):
    spec = P("slab", "member", None)
    return jax.shard_map(
        shards, mesh=mesh, in_specs=(spec, spec, spec), out_specs=spec, check_vma=False
    )
```
